32 devices in a mesh: groups: 2 (over y), cache: 4 (over z), req: 2 (over x), rep: 2 (over core).
Axes of the slice: x: 2, y: 2, z: 4, core: 2. Of those that a mesh axis runs over, the one named last changes fastest.
Arguments:
- candidates: bfloat16 [16, 512, 4, 1024], P(('groups', 'cache', 'req'), None, None, 'rep'), parts along dimension 0, may hold values from -6 to 6
- kv_cache: bfloat16 [256, 2, 64, 1024], P(('groups', 'cache', 'req'), None, None, 'rep'), parts along dimension 0, may hold values from -6 to 6
- tile_owner: int32 [16, 16], P(('groups', 'cache', 'req')), parts along dimension 0, may hold values from 0 to 3, as said below
- tile_slot: int32 [16, 16], P(('groups', 'cache', 'req')), parts along dimension 0, may hold values from 0 to 15
- tile_length: int32 [16, 16], P(('groups', 'cache', 'req')), parts along dimension 0, may hold values from 0 to 64, as said below
- norm_gain: float32 [1024], P('rep'), may hold values from 0.5 to 1.5
Outputs:
- gated: bfloat16 [16, 512, 1024], P(('groups', 'cache', 'req'), None, 'rep'), parts along dimension 0
The draws below stay inside these ranges and needn't reach their ends.
There are 2 independent parts, one for each index of `groups`. The reference program is written for one: setup_inputs(seed, part) draws one part's arguments, and reference() takes and returns one part's arrays. A program takes and returns all parts, laid end to end along the dimension named above; an argument that names none is the same for every part. Nothing has to cross between parts.
Inputs may be any that keep to these rules, and one draw needn't show every extreme that they name: `tile_owner`: among one request's entries of positive tile_length, no owner is named more than 5 times, and one owner exactly 5 times. `tile_length`: an entry of length 0 is padding; every request has an entry of length 64.
All inputs are finite; a program needn't handle non-finite values.
Results may differ from the reference program's by a relative error of at most 0.0066.
Values may be sent and summed in bfloat16 or wider, within the bound.
A program may use at most 64 MiB of HBM per device.

```python
import math
import jax
import jax.numpy as jnp
from jax import lax

D = 1024
HEADS = 8
CAND = 512
TILE = 64
HT = 16
SLOTS = 16
HIST_MAX = 1024
REQS = 8
TILES = 128
N_CACHE = 4
N_REQ = 2


def tile_layout(key):
    shared = jax.random.fold_in(key, 5)
    places = jax.vmap(lambda subkey: jax.random.permutation(subkey, HT))(jax.random.split(shared, REQS))
    groups_of = jnp.where(places == HT - 1, 0, places % N_CACHE)
    return (groups_of, places)


def draw_tile_owner(key, part):
    groups_of, places = tile_layout(key)
    key = jax.random.fold_in(key, 17)
    orders = jax.vmap(lambda subkey: jax.random.permutation(subkey, N_CACHE))(jax.random.split(key, REQS))
    return jnp.take_along_axis(orders, groups_of, axis=1).astype(jnp.int32)


def draw_tile_slot(key, part):
    key = jax.random.fold_in(key, 23)
    return jax.random.randint(key, (REQS, HT), 0, SLOTS, dtype=jnp.int32)


def draw_tile_length(key, part):
    groups_of, places = tile_layout(key)
    key = jax.random.fold_in(key, 29)
    pad_key, keep_key, size_key = jax.random.split(key, 3)
    padding = jax.random.randint(pad_key, (REQS, 1), 0, 3, dtype=jnp.int32)
    keep_roll = jax.random.randint(keep_key, (REQS, HT), 0, 10, dtype=jnp.int32)
    sizes_drawn = jax.random.randint(size_key, (REQS, HT), 1, TILE + 1, dtype=jnp.int32)
    kept = (groups_of == 0) | (keep_roll >= padding)
    lengths = jnp.where(kept, sizes_drawn, 0)
    return jnp.where(places == 0, TILE, lengths).astype(jnp.int32)


def block_levels(rng, dims, pieces, smallest, largest):
    def one(dim, blocks):
        heights = jax.random.uniform(jax.random.fold_in(jax.random.fold_in(rng, 6), dim), (blocks,), jnp.float32, smallest / len(pieces), largest / len(pieces))
        return jnp.repeat(jnp.exp(heights), dims[dim] // blocks).reshape((-1,) + (1,) * (len(dims) - dim - 1))

    loudness = one(*pieces[0])
    for cut in pieces[1:]:
        loudness = loudness * one(*cut)
    return loudness


def scatter_about(key, extent, deviation, limit, cuts=(), kind=jnp.bfloat16):
    gain = block_levels(key, extent, cuts, -0.22, 0.18) if cuts else 1.0
    values = jax.random.normal(key, extent, jnp.float32) * deviation * gain
    return jnp.minimum(jnp.maximum(values, -limit), limit).astype(kind)


def setup_inputs(seed: int = 0, part: int = 0) -> dict:
    key_list = jax.random.split(jax.random.key(seed), 7)
    own_keys = jax.random.split(jax.random.fold_in(key_list[6], part), 7)
    return {
        "candidates": scatter_about(own_keys[0], (REQS, CAND, 4, D), 1.0, 6.0, ((0, 8), (3, 2))),
        "kv_cache": scatter_about(own_keys[1], (TILES, 2, TILE, D), 1.0, 6.0, ((0, 8), (3, 2))),
        "tile_owner": draw_tile_owner(jax.random.fold_in(jax.random.fold_in(key_list[6], part), 71), part),
        "tile_slot": draw_tile_slot(jax.random.fold_in(jax.random.fold_in(key_list[6], part), 71), part),
        "tile_length": draw_tile_length(jax.random.fold_in(jax.random.fold_in(key_list[6], part), 71), part),
        "norm_gain": jnp.clip(1.0 + 0.1 * jax.random.normal(key_list[5], (D,), jnp.float32), 0.5, 1.5),
    }


def reference(candidates, kv_cache, tile_owner, tile_slot, tile_length, norm_gain):
    head_dim = D // HEADS
    scaling = 1.0 / math.sqrt(head_dim)
    positions = jnp.arange(TILE, dtype=jnp.int32)
    gain_row = norm_gain.astype(jnp.float32)

    def per_request(request_item):
        req_index, features, owners, slot_ids, lengths = request_item
        row_index = req_index % N_REQ
        tile_ids = ((owners * N_REQ + row_index) * SLOTS + slot_ids).astype(jnp.int32)
        tile_data = kv_cache[tile_ids]
        key_rows = tile_data[:, 0].reshape(HIST_MAX, HEADS, head_dim).astype(jnp.float32)
        value_rows = tile_data[:, 1].reshape(HIST_MAX, HEADS, head_dim).astype(jnp.float32)
        live_mask = (positions[None, :] < lengths[:, None]).reshape(HIST_MAX).astype(jnp.float32)
        activated = jax.nn.silu(features.astype(jnp.float32)).astype(jnp.bfloat16)
        activated = lax.optimization_barrier(activated).astype(jnp.float32)
        query_rows = activated[:, 0].reshape(CAND, HEADS, head_dim)
        own_key = activated[:, 1].reshape(CAND, HEADS, head_dim)
        own_value = activated[:, 2].reshape(CAND, HEADS, head_dim)
        scores = jnp.einsum('che,khe->hck', query_rows, key_rows) * scaling
        weights = (jax.nn.silu(scores) * live_mask[None, None, :]).astype(jnp.bfloat16)
        weights = lax.optimization_barrier(weights).astype(jnp.float32)
        history = jnp.einsum('hck,khe->che', weights, value_rows)
        own_score = lax.optimization_barrier(jnp.sum(query_rows * own_key, axis=-1)) * scaling
        attended = ((history + jax.nn.silu(own_score)[:, :, None] * own_value) / (HIST_MAX + 1)).reshape(CAND, D)
        average = lax.optimization_barrier(jnp.sum(attended, axis=-1)) / D
        spread = lax.optimization_barrier(jnp.sum(attended * attended, axis=-1)) / D - average * average
        normed = (attended - average[:, None]) * lax.rsqrt(spread[:, None] + 1e-05) * gain_row
        return (normed * activated[:, 3]).astype(jnp.bfloat16)
    return lax.map(per_request, (jnp.arange(REQS, dtype=jnp.int32), candidates, tile_owner, tile_slot, tile_length))
```

```python
import functools
import math

import jax
import jax.numpy as jnp
from jax import lax
from jax.experimental import pallas as pl
from jax.experimental.pallas import tpu as pltpu
from jax.sharding import PartitionSpec as P

D = 1024
HEADS = 8
HEAD = D // HEADS
TILE = 64
HT = 16
HALF_SCALE = 0.5 / math.sqrt(HEAD)
ROWS = 128


def silu_half(half):
    return half + half * jnp.tanh(half)


def kernel(
    n, depth, cand_ref, kv_ref, owner_ref, slot_ref, length_ref, gain_ref, out_ref,
    act, total, stats, peer_stats, table, wanted, wanted_s, own_tiles, outgoing, arrived,
    lens, list_send, list_recv, table_sem, tile_send, tile_recv, stat_send, stat_recv,
):
    me = lax.axis_index("cache")
    core = lax.axis_index("rep")
    cands, width = total.shape
    peers = [lax.rem(me + d, n) for d in range(1, n)]

    barrier = pltpu.get_barrier_semaphore()
    for peer in peers:
        pl.semaphore_signal(
            barrier, inc=1, device_id={"cache": peer}, device_id_type=pl.DeviceIdType.MESH
        )
    pl.semaphore_signal(
        barrier, inc=1, device_id={"rep": 1 - core}, device_id_type=pl.DeviceIdType.MESH
    )

    lane = lax.broadcasted_iota(jnp.int32, (n, 128), 1)
    row = lax.broadcasted_iota(jnp.int32, (n, 128), 0)

    def spread(ref):
        padded = jnp.concatenate([ref[...], jnp.zeros((1, 128 - HT), jnp.int32)], axis=1)
        return jnp.broadcast_to(padded, (n, 128))

    owners, slots, lengths = spread(owner_ref), spread(slot_ref), spread(length_ref)
    owned = ((owners == row) & (lengths > 0)).astype(jnp.int32)
    rank = owned
    for step in (1, 2, 4, 8):
        rank = rank + jnp.where(lane >= step, pltpu.roll(rank, step, 1), 0)
    slot_table = jnp.zeros((n, 128), jnp.int32)
    length_table = jnp.zeros((n, 128), jnp.int32)
    for k in range(depth):
        chosen = (owned > 0) & (rank == k + 1)
        slot_k = jnp.sum(jnp.where(chosen, slots, 0), axis=1, keepdims=True)
        length_k = jnp.sum(jnp.where(chosen, lengths, 0), axis=1, keepdims=True)
        slot_table = jnp.where(lane == k, slot_k, slot_table)
        length_table = jnp.where(lane == k, length_k, length_table)
    for o in range(n):
        table[o] = jnp.broadcast_to(slot_table[o : o + 1], (8, 128))
        lens[o] = jnp.broadcast_to(length_table[o : o + 1], (8, 128))

    pl.semaphore_wait(barrier, n)
    list_copies = []
    for d, peer in enumerate(peers):
        copy = pltpu.make_async_remote_copy(
            src_ref=table.at[peer],
            dst_ref=wanted.at[d],
            send_sem=list_send.at[d],
            recv_sem=list_recv.at[d],
            device_id={"cache": peer},
            device_id_type=pl.DeviceIdType.MESH,
        )
        copy.start()
        list_copies.append(copy)

    tile_copies = {}
    for d, copy in enumerate(list_copies):
        copy.wait_recv()
        to_scalar = pltpu.make_async_copy(wanted.at[d], wanted_s.at[d], table_sem.at[d])
        to_scalar.start()
    own_scalar = pltpu.make_async_copy(table.at[me], wanted_s.at[n - 1], table_sem.at[n - 1])
    own_scalar.start()
    for d in range(n - 1):
        pltpu.make_async_copy(wanted.at[d], wanted_s.at[d], table_sem.at[d]).wait()
    own_scalar.wait()
    for k in range(depth):
        for d in range(n - 1):
            home = lax.rem(me + n - d - 1, n)
            outgoing[k, d] = kv_ref[wanted_s[d, 0, k]]
            copy = pltpu.make_async_remote_copy(
                src_ref=outgoing.at[k, d],
                dst_ref=arrived.at[k, d],
                send_sem=tile_send.at[k, d],
                recv_sem=tile_recv.at[k, d],
                device_id={"cache": home},
                device_id_type=pl.DeviceIdType.MESH,
            )
            copy.start()
            tile_copies[k, d] = copy

    def activate(block, carry):
        rows = pl.ds(pl.multiple_of(block * ROWS, ROWS), ROWS)
        for i in range(4):
            half = cand_ref[0, rows, i, :].astype(jnp.float32) * 0.5
            act[i, rows, :] = silu_half(half).astype(jnp.bfloat16)
        for h in range(width // HEAD):
            cols = slice(h * HEAD, (h + 1) * HEAD)
            query = act[0, rows, cols].astype(jnp.float32)
            key = act[1, rows, cols].astype(jnp.float32)
            value = act[2, rows, cols].astype(jnp.float32)
            score = jnp.sum(query * key, axis=1, keepdims=True)
            total[rows, cols] = silu_half(score * HALF_SCALE) * value
        return carry

    lax.fori_loop(0, cands // ROWS, activate, 0)

    for k in range(depth):
        own_tiles[k] = kv_ref[wanted_s[n - 1, 0, k]]

    position = lax.broadcasted_iota(jnp.int32, (TILE, width), 0)

    def attend(tiles, counts, tile_count):
        for t in range(tile_count):
            live = (position < counts[t]).astype(jnp.float32)
            tiles[t, 0] = (tiles[t, 0].astype(jnp.float32) * live).astype(jnp.bfloat16)

        def one(block, carry):
            rows = pl.ds(pl.multiple_of(block * ROWS, ROWS), ROWS)
            for h in range(width // HEAD):
                cols = slice(h * HEAD, (h + 1) * HEAD)
                keys = tiles[:, 0, :, cols].reshape(tile_count * TILE, HEAD)
                values = tiles[:, 1, :, cols].reshape(tile_count * TILE, HEAD)
                scores = lax.dot_general(
                    act[0, rows, cols], keys, (((1,), (1,)), ((), ())),
                    preferred_element_type=jnp.float32,
                )
                weights = silu_half(scores * HALF_SCALE).astype(jnp.bfloat16)
                total[rows, cols] += jnp.dot(
                    weights, values, preferred_element_type=jnp.float32
                )
            return carry

        lax.fori_loop(0, cands // ROWS, one, 0)

    own_counts = lens[me]
    attend(own_tiles, [own_counts[0:1, k : k + 1] for k in range(depth)], depth)
    for k in range(depth):
        counts = []
        for d in range(n - 1):
            tile_copies[k, d].wait_recv()
            counts.append(lens[lax.rem(me + d + 1, n)][0:1, k : k + 1])
        attend(arrived.at[k], counts, n - 1)

    def moments(block, carry):
        rows = pl.ds(pl.multiple_of(block * ROWS, ROWS), ROWS)
        attended = total[rows, :] * (1.0 / (HT * TILE + 1))
        sums = jnp.sum(attended, axis=1, keepdims=True)
        squares = jnp.sum(attended * attended, axis=1, keepdims=True)
        at = lax.broadcasted_iota(jnp.int32, (ROWS, 128), 1)
        stats[rows, :] = jnp.where(at < 64, sums, squares)
        return carry

    lax.fori_loop(0, cands // ROWS, moments, 0)
    stat_copy = pltpu.make_async_remote_copy(
        src_ref=stats,
        dst_ref=peer_stats,
        send_sem=stat_send,
        recv_sem=stat_recv,
        device_id={"rep": 1 - core},
        device_id_type=pl.DeviceIdType.MESH,
    )
    stat_copy.start()
    stat_copy.wait_recv()

    def finish(block, carry):
        rows = pl.ds(pl.multiple_of(block * ROWS, ROWS), ROWS)
        both = stats[rows, :] + peer_stats[rows, :]
        average = both[:, 0:1] * (1.0 / D)
        spread_ = both[:, 64:65] * (1.0 / D) - average * average
        attended = total[rows, :] * (1.0 / (HT * TILE + 1))
        normed = (attended - average) * lax.rsqrt(spread_ + 1e-05) * gain_ref[...]
        out_ref[0, rows, :] = (normed * act[3, rows, :].astype(jnp.float32)).astype(jnp.bfloat16)
        return carry

    lax.fori_loop(0, cands // ROWS, finish, 0)
    stat_copy.wait_send()
    for copy in list_copies:
        copy.wait_send()
    for copy in tile_copies.values():
        copy.wait_send()


def local(candidates, kv_cache, tile_owner, tile_slot, tile_length, norm_gain):
    n = lax.axis_size("cache")
    depth = (HT - 2) // n + 2
    cands, width = candidates.shape[1], candidates.shape[3]
    vmem = pl.BlockSpec(memory_space=pltpu.VMEM)
    tile = (2, TILE, width)
    dma = pltpu.SemaphoreType.DMA
    return pl.pallas_call(
        functools.partial(kernel, n, depth),
        out_shape=jax.ShapeDtypeStruct((1, cands, width), jnp.bfloat16),
        in_specs=[vmem] * 6,
        out_specs=vmem,
        scratch_shapes=[
            pltpu.VMEM((4, cands, width), jnp.bfloat16),
            pltpu.VMEM((cands, width), jnp.float32),
            pltpu.VMEM((cands, 128), jnp.float32),
            pltpu.VMEM((cands, 128), jnp.float32),
            pltpu.VMEM((n, 8, 128), jnp.int32),
            pltpu.VMEM((n - 1, 8, 128), jnp.int32),
            pltpu.SMEM((n, 8, 128), jnp.int32),
            pltpu.VMEM((depth,) + tile, jnp.bfloat16),
            pltpu.VMEM((depth, n - 1) + tile, jnp.bfloat16),
            pltpu.VMEM((depth, n - 1) + tile, jnp.bfloat16),
            pltpu.VMEM((n, 8, 128), jnp.int32),
            dma((n - 1,)),
            dma((n - 1,)),
            dma((n,)),
            dma((depth, n - 1)),
            dma((depth, n - 1)),
            dma,
            dma,
        ],
        compiler_params=pltpu.CompilerParams(
            collective_id=0, has_side_effects=True, vmem_limit_bytes=48 * 1024 * 1024
        ),
        cost_estimate=pl.CostEstimate(
            flops=4 * cands * width * HT * TILE, bytes_accessed=5 * 2**20, transcendentals=0
        ),
    )(candidates, kv_cache, tile_owner, tile_slot, tile_length, norm_gain[None])


def solution(mesh):
    placed = (
        P(("groups", "cache", "req"), None, None, "rep"),
        P(("groups", "cache", "req"), None, None, "rep"),
        P(("groups", "cache", "req"), None),
        P(("groups", "cache", "req"), None),
        P(("groups", "cache", "req"), None),
        P("rep"),
    )
    return jax.shard_map(
        local,
        mesh=mesh,
        in_specs=placed,
        out_specs=P(("groups", "cache", "req"), None, "rep"),
        check_vma=False,
    )
```

```python
import functools
import math

import jax
import jax.numpy as jnp
from jax import lax
from jax.experimental import pallas as pl
from jax.experimental.pallas import tpu as pltpu
from jax.sharding import PartitionSpec as P

D = 1024
HEADS = 8
HEAD = D // HEADS
TILE = 64
HT = 16
HALF_SCALE = 0.5 / math.sqrt(HEAD)
ROWS = 128


def silu_half(half):
    return half + half * jnp.tanh(half)


def kernel(
    n, depth, split, cand_hbm, kv_hbm, owner_hbm, slot_hbm, length_hbm, gain_hbm, out_ref,
    cand_ref, kv_ref, lists, gain_ref,
    act, total, stats, peer_stats, table, wanted, wanted_s, own_tiles, outgoing, arrived,
    peer_query, peer_total, partial_out, partial_in,
    load_sem, list_send, list_recv, table_sem, tile_send, tile_recv, stat_send, stat_recv,
    query_send, query_recv, partial_send, partial_recv,
):
    me = lax.axis_index("cache")
    core = lax.axis_index("rep")
    cands, width = total.shape
    peers = [lax.rem(me + d, n) for d in range(1, n)]
    middle = (me + 1) // 2 == 1
    edge = (me + 1) // 2 != 1
    near = 4 - 2 * me

    list_loads = [
        pltpu.make_async_copy(src, lists.at[i], load_sem.at[i])
        for i, src in enumerate((owner_hbm, slot_hbm, length_hbm))
    ]
    cand_load = pltpu.make_async_copy(cand_hbm.at[0], cand_ref, load_sem.at[3])
    kv_load = pltpu.make_async_copy(kv_hbm, kv_ref, load_sem.at[4])
    gain_load = pltpu.make_async_copy(gain_hbm, gain_ref, load_sem.at[5])
    for load in list_loads + [cand_load, kv_load, gain_load]:
        load.start()

    barrier = pltpu.get_barrier_semaphore()
    for peer in peers:
        pl.semaphore_signal(
            barrier, inc=1, device_id={"cache": peer}, device_id_type=pl.DeviceIdType.MESH
        )
    pl.semaphore_signal(
        barrier, inc=1, device_id={"rep": 1 - core}, device_id_type=pl.DeviceIdType.MESH
    )
    for load in list_loads:
        load.wait()

    lane = lax.broadcasted_iota(jnp.int32, (n, 128), 1)
    row = lax.broadcasted_iota(jnp.int32, (n, 128), 0)

    def spread(i):
        padded = jnp.concatenate([lists[i], jnp.zeros((1, 128 - HT), jnp.int32)], axis=1)
        return jnp.broadcast_to(padded, (n, 128))

    owners, slots, lengths = spread(0), spread(1), spread(2)
    owned = ((owners == row) & (lengths > 0) & (lane < HT)).astype(jnp.int32)
    rank = owned
    for step in (1, 2, 4, 8):
        rank = rank + jnp.where(lane >= step, pltpu.roll(rank, step, 1), 0)
    slot_table = jnp.zeros((n, 128), jnp.int32)
    length_table = jnp.zeros((n, 128), jnp.int32)
    for k in range(depth):
        chosen = (owned > 0) & (rank == k + 1)
        slot_k = jnp.sum(jnp.where(chosen, slots, 0), axis=1, keepdims=True)
        length_k = jnp.sum(jnp.where(chosen, lengths, 0), axis=1, keepdims=True)
        slot_table = jnp.where(lane == k, slot_k, slot_table)
        length_table = jnp.where(lane == k, length_k, length_table)
    line = lax.broadcasted_iota(jnp.int32, (8, 128), 0)
    for o in range(n):
        table[o] = jnp.where(line == 0, slot_table[o : o + 1], length_table[o : o + 1])

    pl.semaphore_wait(barrier, n)
    list_copies = []
    for d, peer in enumerate(peers):
        copy = pltpu.make_async_remote_copy(
            src_ref=table,
            dst_ref=wanted.at[d],
            send_sem=list_send.at[d],
            recv_sem=list_recv.at[d],
            device_id={"cache": peer},
            device_id_type=pl.DeviceIdType.MESH,
        )
        copy.start()
        list_copies.append(copy)
    own_scalar = pltpu.make_async_copy(table.at[me], wanted_s.at[n - 1], table_sem.at[n - 1])
    own_scalar.start()

    def activate(parts):
        def one(block, carry):
            rows = pl.ds(pl.multiple_of(block * ROWS, ROWS), ROWS)
            for i in parts:
                half = cand_ref[rows, i, :].astype(jnp.float32) * 0.5
                act[i, rows, :] = silu_half(half).astype(jnp.bfloat16)
            return carry

        lax.fori_loop(0, cands // ROWS, one, 0)

    cand_load.wait()
    query_copy = pltpu.make_async_remote_copy(
        src_ref=act.at[0],
        dst_ref=peer_query,
        send_sem=query_send,
        recv_sem=query_recv,
        device_id={"cache": lax.rem(n + 3 - me, n)},
        device_id_type=pl.DeviceIdType.MESH,
    )
    partial_copy = pltpu.make_async_remote_copy(
        src_ref=partial_out,
        dst_ref=partial_in,
        send_sem=partial_send,
        recv_sem=partial_recv,
        device_id={"cache": lax.rem(n + 3 - me, n)},
        device_id_type=pl.DeviceIdType.MESH,
    )
    if split:
        activate((0,))
        pl.when(middle)(query_copy.start)

    to_scalar = []
    for d, copy in enumerate(list_copies):
        copy.wait_recv()
        move = pltpu.make_async_copy(wanted.at[d, me], wanted_s.at[d], table_sem.at[d])
        move.start()
        to_scalar.append(move)
    kv_load.wait()
    for move in to_scalar:
        move.wait()
    own_scalar.wait()

    def tile_copy(k, d):
        to = lax.rem(me + n - d - 1, n)
        if split and d == 1:
            to = jnp.where(edge, 1 + me // 2, to)
        return pltpu.make_async_remote_copy(
            src_ref=outgoing.at[k, d],
            dst_ref=arrived.at[k, d],
            send_sem=tile_send.at[k, d],
            recv_sem=tile_recv.at[k, d],
            device_id={"cache": to},
            device_id_type=pl.DeviceIdType.MESH,
        )

    def push(k, d):
        outgoing[k, d] = kv_ref[wanted_s[d, 0, k]]
        tile_copy(k, d).start()

    def is_sent(d):
        return jnp.logical_or(me != 1 if d == 2 else me != 2, edge)

    if split:
        for k in range(depth):
            push(k, 1)
        for k in range(depth):
            for d in (0, 2):
                pl.when(is_sent(d))(functools.partial(push, k, d))
    else:
        for k in range(depth):
            for d in range(n - 1):
                push(k, d)

    activate((1, 2, 3) if split else (0, 1, 2, 3))

    def own_term(block, carry):
        rows = pl.ds(pl.multiple_of(block * ROWS, ROWS), ROWS)
        for h in range(width // HEAD):
            cols = slice(h * HEAD, (h + 1) * HEAD)
            query = act[0, rows, cols].astype(jnp.float32)
            key = act[1, rows, cols].astype(jnp.float32)
            value = act[2, rows, cols].astype(jnp.float32)
            score = jnp.sum(query * key, axis=1, keepdims=True)
            total[rows, cols] = silu_half(score * HALF_SCALE) * value
        return carry

    lax.fori_loop(0, cands // ROWS, own_term, 0)
    position = lax.broadcasted_iota(jnp.int32, (TILE, width), 0)

    def attend(query, result, tiles, counts, first=False):
        tile_count = len(counts)
        for t in range(tile_count):
            live = (position < counts[t]).astype(jnp.float32)
            tiles[t, 0] = (tiles[t, 0].astype(jnp.float32) * live).astype(jnp.bfloat16)

        def one(block, carry):
            rows = pl.ds(pl.multiple_of(block * ROWS, ROWS), ROWS)
            for h in range(width // HEAD):
                cols = slice(h * HEAD, (h + 1) * HEAD)
                keys = tiles[:, 0, :, cols].reshape(tile_count * TILE, HEAD)
                values = tiles[:, 1, :, cols].reshape(tile_count * TILE, HEAD)
                scores = lax.dot_general(
                    query[rows, cols], keys, (((1,), (1,)), ((), ())),
                    preferred_element_type=jnp.float32,
                )
                weights = silu_half(scores * HALF_SCALE).astype(jnp.bfloat16)
                added = jnp.dot(weights, values, preferred_element_type=jnp.float32)
                result[rows, cols] = added if first else result[rows, cols] + added
            return carry

        lax.fori_loop(0, cands // ROWS, one, 0)

    def counts_of(ref):
        block = ref[...]
        return [block[1:2, k : k + 1] for k in range(depth)]

    for k in range(depth):
        own_tiles[k] = kv_ref[wanted_s[n - 1, 0, k]]
    attend(act.at[0], total, own_tiles, counts_of(table.at[me]))

    def from_all():
        for k in range(depth):
            counts = []
            for d in range(n - 1):
                tile_copy(k, d).wait_recv()
                counts.append(table[lax.rem(me + d + 1, n)][1:2, k : k + 1])
            attend(act.at[0], total, arrived.at[k], counts)

    def for_both():
        side = 3 * (me - 1)
        for k in range(depth):
            own_tiles[k] = kv_ref[wanted_s[near, 0, k]]
        query_copy.wait_recv()
        attend(peer_query, peer_total, own_tiles, counts_of(wanted.at[near, me]), first=True)
        for k in range(depth):
            tile_copy(k, 1).wait_recv()
        attend(peer_query, peer_total, arrived.at[:, 1], counts_of(wanted.at[near, side]))

        def narrow(block, carry):
            rows = pl.ds(pl.multiple_of(block * ROWS, ROWS), ROWS)
            partial_out[rows, :] = peer_total[rows, :].astype(jnp.bfloat16)
            return carry

        lax.fori_loop(0, cands // ROWS, narrow, 0)
        partial_copy.start()
        for d in (0, 2):

            @pl.when(near == d)
            def _():
                for k in range(depth):
                    tile_copy(k, d).wait_recv()
                attend(act.at[0], total, arrived.at[:, d], counts_of(table.at[side]))

        partial_copy.wait_recv()

        def widen(block, carry):
            rows = pl.ds(pl.multiple_of(block * ROWS, ROWS), ROWS)
            total[rows, :] += partial_in[rows, :].astype(jnp.float32)
            return carry

        lax.fori_loop(0, cands // ROWS, widen, 0)

    if split:
        pl.when(edge)(from_all)
        pl.when(middle)(for_both)
    else:
        from_all()

    gain_load.wait()

    def moments(block, carry):
        rows = pl.ds(pl.multiple_of(block * ROWS, ROWS), ROWS)
        attended = total[rows, :] * (1.0 / (HT * TILE + 1))
        sums = jnp.sum(attended, axis=1, keepdims=True)
        squares = jnp.sum(attended * attended, axis=1, keepdims=True)
        at = lax.broadcasted_iota(jnp.int32, (ROWS, 128), 1)
        stats[rows, :] = jnp.where(at < 64, sums, squares)
        return carry

    lax.fori_loop(0, cands // ROWS, moments, 0)
    stat_copy = pltpu.make_async_remote_copy(
        src_ref=stats,
        dst_ref=peer_stats,
        send_sem=stat_send,
        recv_sem=stat_recv,
        device_id={"rep": 1 - core},
        device_id_type=pl.DeviceIdType.MESH,
    )
    stat_copy.start()
    stat_copy.wait_recv()

    def finish(block, carry):
        rows = pl.ds(pl.multiple_of(block * ROWS, ROWS), ROWS)
        both = stats[rows, :] + peer_stats[rows, :]
        average = both[:, 0:1] * (1.0 / D)
        variance = both[:, 64:65] * (1.0 / D) - average * average
        attended = total[rows, :] * (1.0 / (HT * TILE + 1))
        normed = (attended - average) * lax.rsqrt(variance + 1e-05) * gain_ref[...]
        out_ref[0, rows, :] = (normed * act[3, rows, :].astype(jnp.float32)).astype(jnp.bfloat16)
        return carry

    lax.fori_loop(0, cands // ROWS, finish, 0)
    stat_copy.wait_send()
    for copy in list_copies:
        copy.wait_send()
    for k in range(depth):
        for d in range(n - 1):
            wait = tile_copy(k, d).wait_send
            if split and d != 1:
                pl.when(is_sent(d))(wait)
            else:
                wait()
    if split:

        @pl.when(middle)
        def _():
            query_copy.wait_send()
            partial_copy.wait_send()


def local(candidates, kv_cache, tile_owner, tile_slot, tile_length, norm_gain):
    n = lax.axis_size("cache")
    depth = (HT - 2) // n + 2
    cands, width = candidates.shape[1], candidates.shape[3]
    vmem = pl.BlockSpec(memory_space=pltpu.VMEM)
    tile = (2, TILE, width)
    dma = pltpu.SemaphoreType.DMA
    return pl.pallas_call(
        functools.partial(kernel, n, depth, n == 4),
        out_shape=jax.ShapeDtypeStruct((1, cands, width), jnp.bfloat16),
        in_specs=[pl.BlockSpec(memory_space=pltpu.HBM)] * 6,
        out_specs=vmem,
        scratch_shapes=[
            pltpu.VMEM((cands, 4, width), jnp.bfloat16),
            pltpu.VMEM(kv_cache.shape, jnp.bfloat16),
            pltpu.VMEM((3, 1, HT), jnp.int32),
            pltpu.VMEM((1, width), jnp.float32),
            pltpu.VMEM((4, cands, width), jnp.bfloat16),
            pltpu.VMEM((cands, width), jnp.float32),
            pltpu.VMEM((cands, 128), jnp.float32),
            pltpu.VMEM((cands, 128), jnp.float32),
            pltpu.VMEM((n, 8, 128), jnp.int32),
            pltpu.VMEM((n - 1, n, 8, 128), jnp.int32),
            pltpu.SMEM((n, 8, 128), jnp.int32),
            pltpu.VMEM((depth,) + tile, jnp.bfloat16),
            pltpu.VMEM((depth, n - 1) + tile, jnp.bfloat16),
            pltpu.VMEM((depth, n - 1) + tile, jnp.bfloat16),
            pltpu.VMEM((cands, width), jnp.bfloat16),
            pltpu.VMEM((cands, width), jnp.float32),
            pltpu.VMEM((cands, width), jnp.bfloat16),
            pltpu.VMEM((cands, width), jnp.bfloat16),
            dma((6,)),
            dma((n - 1,)),
            dma((n - 1,)),
            dma((n,)),
            dma((depth, n - 1)),
            dma((depth, n - 1)),
            dma,
            dma,
            dma,
            dma,
            dma,
            dma,
        ],
        compiler_params=pltpu.CompilerParams(
            collective_id=0, has_side_effects=True, vmem_limit_bytes=48 * 1024 * 1024
        ),
        cost_estimate=pl.CostEstimate(
            flops=4 * cands * width * HT * TILE, bytes_accessed=5 * 2**20, transcendentals=0
        ),
    )(candidates, kv_cache, tile_owner, tile_slot, tile_length, norm_gain[None])


def solution(mesh):
    placed = (
        P(("groups", "cache", "req"), None, None, "rep"),
        P(("groups", "cache", "req"), None, None, "rep"),
        P(("groups", "cache", "req"), None),
        P(("groups", "cache", "req"), None),
        P(("groups", "cache", "req"), None),
        P("rep"),
    )
    return jax.shard_map(
        local,
        mesh=mesh,
        in_specs=placed,
        out_specs=P(("groups", "cache", "req"), None, "rep"),
        check_vma=False,
    )
```

```python
import functools
import math

import jax
import jax.numpy as jnp
from jax import lax
from jax.experimental import pallas as pl
from jax.experimental.pallas import tpu as pltpu
from jax.sharding import PartitionSpec as P

D = 1024
HEADS = 8
HEAD = D // HEADS
TILE = 64
HT = 16
HALF_SCALE = 0.5 / math.sqrt(HEAD)
ROWS = 128


def silu_half(half):
    return half + half * jnp.tanh(half)


def kernel(
    n, depth, split, cand_hbm, kv_hbm, owner_hbm, slot_hbm, length_hbm, gain_hbm, out_ref,
    cand_ref, kv_ref, lists, gain_ref,
    act, total, stats, peer_stats, table, wanted, wanted_s, own_tiles, outgoing, arrived,
    peer_query, peer_total, partial_out, partial_in,
    load_sem, list_send, list_recv, table_sem, tile_send, tile_recv, stat_send, stat_recv,
    query_send, query_recv, partial_send, partial_recv,
):
    me = lax.axis_index("cache")
    core = lax.axis_index("rep")
    cands, width = total.shape
    peers = [lax.rem(me + d, n) for d in range(1, n)]
    middle = (me + 1) // 2 == 1
    edge = (me + 1) // 2 != 1
    near = 4 - 2 * me

    list_loads = [
        pltpu.make_async_copy(src, lists.at[i], load_sem.at[i])
        for i, src in enumerate((owner_hbm, slot_hbm, length_hbm))
    ]
    cand_load = pltpu.make_async_copy(cand_hbm.at[0], cand_ref, load_sem.at[3])
    kv_load = pltpu.make_async_copy(kv_hbm, kv_ref, load_sem.at[4])
    gain_load = pltpu.make_async_copy(gain_hbm, gain_ref, load_sem.at[5])
    for load in list_loads + [cand_load, kv_load, gain_load]:
        load.start()

    barrier = pltpu.get_barrier_semaphore()
    for peer in peers:
        pl.semaphore_signal(
            barrier, inc=1, device_id={"cache": peer}, device_id_type=pl.DeviceIdType.MESH
        )
    pl.semaphore_signal(
        barrier, inc=1, device_id={"rep": 1 - core}, device_id_type=pl.DeviceIdType.MESH
    )
    for load in list_loads:
        load.wait()

    lane = lax.broadcasted_iota(jnp.int32, (n, 128), 1)
    row = lax.broadcasted_iota(jnp.int32, (n, 128), 0)

    def spread(i):
        padded = jnp.concatenate([lists[i], jnp.zeros((1, 128 - HT), jnp.int32)], axis=1)
        return jnp.broadcast_to(padded, (n, 128))

    owners, slots, lengths = spread(0), spread(1), spread(2)
    owned = ((owners == row) & (lengths > 0) & (lane < HT)).astype(jnp.int32)
    rank = owned
    for step in (1, 2, 4, 8):
        rank = rank + jnp.where(lane >= step, pltpu.roll(rank, step, 1), 0)
    slot_table = jnp.zeros((n, 128), jnp.int32)
    length_table = jnp.zeros((n, 128), jnp.int32)
    for k in range(depth):
        chosen = (owned > 0) & (rank == k + 1)
        slot_k = jnp.sum(jnp.where(chosen, slots, 0), axis=1, keepdims=True)
        length_k = jnp.sum(jnp.where(chosen, lengths, 0), axis=1, keepdims=True)
        slot_table = jnp.where(lane == k, slot_k, slot_table)
        length_table = jnp.where(lane == k, length_k, length_table)
    line = lax.broadcasted_iota(jnp.int32, (8, 128), 0)
    for o in range(n):
        table[o] = jnp.where(line == 0, slot_table[o : o + 1], length_table[o : o + 1])

    pl.semaphore_wait(barrier, n)
    list_copies = []
    for d, peer in enumerate(peers):
        copy = pltpu.make_async_remote_copy(
            src_ref=table,
            dst_ref=wanted.at[d],
            send_sem=list_send.at[d],
            recv_sem=list_recv.at[d],
            device_id={"cache": peer},
            device_id_type=pl.DeviceIdType.MESH,
        )
        copy.start()
        list_copies.append(copy)
    own_scalar = pltpu.make_async_copy(table.at[me], wanted_s.at[n - 1], table_sem.at[n - 1])
    own_scalar.start()

    def activate(parts):
        def one(block, carry):
            rows = pl.ds(pl.multiple_of(block * ROWS, ROWS), ROWS)
            for i in parts:
                half = cand_ref[rows, i, :].astype(jnp.float32) * 0.5
                act[i, rows, :] = silu_half(half).astype(jnp.bfloat16)
            return carry

        lax.fori_loop(0, cands // ROWS, one, 0)

    cand_load.wait()
    query_copy = pltpu.make_async_remote_copy(
        src_ref=act.at[0],
        dst_ref=peer_query,
        send_sem=query_send,
        recv_sem=query_recv,
        device_id={"cache": lax.rem(n + 3 - me, n)},
        device_id_type=pl.DeviceIdType.MESH,
    )
    partial_copy = pltpu.make_async_remote_copy(
        src_ref=partial_out,
        dst_ref=partial_in,
        send_sem=partial_send,
        recv_sem=partial_recv,
        device_id={"cache": lax.rem(n + 3 - me, n)},
        device_id_type=pl.DeviceIdType.MESH,
    )
    if split:
        activate((0,))
        pl.when(middle)(query_copy.start)

    to_scalar = []
    for d, copy in enumerate(list_copies):
        copy.wait_recv()
        move = pltpu.make_async_copy(wanted.at[d, me], wanted_s.at[d], table_sem.at[d])
        move.start()
        to_scalar.append(move)
    kv_load.wait()
    for move in to_scalar:
        move.wait()
    own_scalar.wait()

    def tile_copy(k, d):
        to = lax.rem(me + n - d - 1, n)
        if split and d == 1:
            to = jnp.where(edge, 1 + me // 2, to)
        return pltpu.make_async_remote_copy(
            src_ref=outgoing.at[k, d],
            dst_ref=arrived.at[k, d],
            send_sem=tile_send.at[k, d],
            recv_sem=tile_recv.at[k, d],
            device_id={"cache": to},
            device_id_type=pl.DeviceIdType.MESH,
        )

    def push(k, d):
        outgoing[k, d] = kv_ref[wanted_s[d, 0, k]]
        tile_copy(k, d).start()

    def is_sent(d):
        return jnp.logical_or(me != 1 if d == 2 else me != 2, edge)

    if split:
        for k in range(depth):
            push(k, 1)
        for k in range(depth):
            for d in (0, 2):
                pl.when(is_sent(d))(functools.partial(push, k, d))
    else:
        for k in range(depth):
            for d in range(n - 1):
                push(k, d)

    activate((1, 2, 3) if split else (0, 1, 2, 3))

    def own_term(block, carry):
        rows = pl.ds(pl.multiple_of(block * ROWS, ROWS), ROWS)
        for h in range(width // HEAD):
            cols = slice(h * HEAD, (h + 1) * HEAD)
            query = act[0, rows, cols].astype(jnp.float32)
            key = act[1, rows, cols].astype(jnp.float32)
            value = act[2, rows, cols].astype(jnp.float32)
            score = jnp.sum(query * key, axis=1, keepdims=True)
            total[rows, cols] = silu_half(score * HALF_SCALE) * value
        return carry

    lax.fori_loop(0, cands // ROWS, own_term, 0)
    position = lax.broadcasted_iota(jnp.int32, (TILE, width), 0)

    def attend(query, result, tiles, counts, first=False):
        tile_count = len(counts)
        for t in range(tile_count):
            live = (position < counts[t]).astype(jnp.float32)
            tiles[t, 0] = (tiles[t, 0].astype(jnp.float32) * live).astype(jnp.bfloat16)

        def one(block, carry):
            rows = pl.ds(pl.multiple_of(block * ROWS, ROWS), ROWS)
            for h in range(width // HEAD):
                cols = slice(h * HEAD, (h + 1) * HEAD)
                keys = tiles[:, 0, :, cols].reshape(tile_count * TILE, HEAD)
                values = tiles[:, 1, :, cols].reshape(tile_count * TILE, HEAD)
                scores = lax.dot_general(
                    query[rows, cols], keys, (((1,), (1,)), ((), ())),
                    preferred_element_type=jnp.float32,
                )
                weights = silu_half(scores * HALF_SCALE).astype(jnp.bfloat16)
                added = jnp.dot(weights, values, preferred_element_type=jnp.float32)
                result[rows, cols] = added if first else result[rows, cols] + added
            return carry

        lax.fori_loop(0, cands // ROWS, one, 0)

    def counts_of(ref):
        block = ref[...]
        return [block[1:2, k : k + 1] for k in range(depth)]

    for k in range(depth):
        own_tiles[k] = kv_ref[wanted_s[n - 1, 0, k]]
    attend(act.at[0], total, own_tiles, counts_of(table.at[me]))

    def from_all():
        for k in range(depth):
            counts = []
            for d in range(n - 1):
                tile_copy(k, d).wait_recv()
                counts.append(table[lax.rem(me + d + 1, n)][1:2, k : k + 1])
            attend(act.at[0], total, arrived.at[k], counts)

    def for_both():
        side = 3 * (me - 1)
        for k in range(depth):
            own_tiles[k] = kv_ref[wanted_s[near, 0, k]]
        query_copy.wait_recv()
        attend(peer_query, peer_total, own_tiles, counts_of(wanted.at[near, me]), first=True)
        for k in range(depth):
            tile_copy(k, 1).wait_recv()
        attend(peer_query, peer_total, arrived.at[:, 1], counts_of(wanted.at[near, side]))

        def narrow(block, carry):
            rows = pl.ds(pl.multiple_of(block * ROWS, ROWS), ROWS)
            partial_out[rows, :] = peer_total[rows, :].astype(jnp.bfloat16)
            return carry

        lax.fori_loop(0, cands // ROWS, narrow, 0)
        partial_copy.start()
        for d in (0, 2):

            @pl.when(near == d)
            def _():
                for k in range(depth):
                    tile_copy(k, d).wait_recv()
                attend(act.at[0], total, arrived.at[:, d], counts_of(table.at[side]))

        partial_copy.wait_recv()

        def widen(block, carry):
            rows = pl.ds(pl.multiple_of(block * ROWS, ROWS), ROWS)
            total[rows, :] += partial_in[rows, :].astype(jnp.float32)
            return carry

        lax.fori_loop(0, cands // ROWS, widen, 0)

    if split:
        pl.when(edge)(from_all)
        pl.when(middle)(for_both)
    else:
        from_all()

    gain_load.wait()

    def moments(block, carry):
        rows = pl.ds(pl.multiple_of(block * ROWS, ROWS), ROWS)
        attended = total[rows, :] * (1.0 / (HT * TILE + 1))
        sums = jnp.sum(attended, axis=1, keepdims=True)
        squares = jnp.sum(attended * attended, axis=1, keepdims=True)
        at = lax.broadcasted_iota(jnp.int32, (ROWS, 128), 1)
        stats[rows, :] = jnp.where(at < 64, sums, squares)
        return carry

    lax.fori_loop(0, cands // ROWS, moments, 0)
    stat_copy = pltpu.make_async_remote_copy(
        src_ref=stats,
        dst_ref=peer_stats,
        send_sem=stat_send,
        recv_sem=stat_recv,
        device_id={"rep": 1 - core},
        device_id_type=pl.DeviceIdType.MESH,
    )
    stat_copy.start()
    stat_copy.wait_recv()

    def finish(block, carry):
        rows = pl.ds(pl.multiple_of(block * ROWS, ROWS), ROWS)
        both = stats[rows, :] + peer_stats[rows, :]
        average = both[:, 0:1] * (1.0 / D)
        variance = both[:, 64:65] * (1.0 / D) - average * average
        attended = total[rows, :] * (1.0 / (HT * TILE + 1))
        normed = (attended - average) * lax.rsqrt(variance + 1e-05) * gain_ref[...]
        out_ref[0, rows, :] = (normed * act[3, rows, :].astype(jnp.float32)).astype(jnp.bfloat16)
        return carry

    lax.fori_loop(0, cands // ROWS, finish, 0)
    stat_copy.wait_send()
    for copy in list_copies:
        copy.wait_send()
    for k in range(depth):
        for d in range(n - 1):
            wait = tile_copy(k, d).wait_send
            if split and d != 1:
                pl.when(is_sent(d))(wait)
            else:
                wait()
    if split:

        @pl.when(middle)
        def _():
            query_copy.wait_send()
            partial_copy.wait_send()


def local(candidates, kv_cache, tile_owner, tile_slot, tile_length, norm_gain):
    n = lax.axis_size("cache")
    depth = (HT - 2) // n + 2
    cands, width = candidates.shape[1], candidates.shape[3]
    vmem = pl.BlockSpec(memory_space=pltpu.VMEM)
    tile = (2, TILE, width)
    dma = pltpu.SemaphoreType.DMA
    return pl.pallas_call(
        functools.partial(kernel, n, depth, n == 4),
        out_shape=jax.ShapeDtypeStruct((1, cands, width), jnp.bfloat16),
        in_specs=[pl.BlockSpec(memory_space=pltpu.HBM)] * 6,
        out_specs=vmem,
        scratch_shapes=[
            pltpu.VMEM((cands, 4, width), jnp.bfloat16),
            pltpu.VMEM(kv_cache.shape, jnp.bfloat16),
            pltpu.VMEM((3, 1, HT), jnp.int32),
            pltpu.VMEM((1, width), jnp.float32),
            pltpu.VMEM((4, cands, width), jnp.bfloat16),
            pltpu.VMEM((cands, width), jnp.float32),
            pltpu.VMEM((cands, 128), jnp.float32),
            pltpu.VMEM((cands, 128), jnp.float32),
            pltpu.VMEM((n, 8, 128), jnp.int32),
            pltpu.VMEM((n - 1, n, 8, 128), jnp.int32),
            pltpu.SMEM((n, 8, 128), jnp.int32),
            pltpu.VMEM((depth,) + tile, jnp.bfloat16),
            pltpu.VMEM((depth, n - 1) + tile, jnp.bfloat16),
            pltpu.VMEM((depth, n - 1) + tile, jnp.bfloat16),
            pltpu.VMEM((cands, width), jnp.bfloat16),
            pltpu.VMEM((cands, width), jnp.float32),
            pltpu.VMEM((cands, width), jnp.bfloat16),
            pltpu.VMEM((cands, width), jnp.bfloat16),
            dma((6,)),
            dma((n - 1,)),
            dma((n - 1,)),
            dma((n,)),
            dma((depth, n - 1)),
            dma((depth, n - 1)),
            dma,
            dma,
            dma,
            dma,
            dma,
            dma,
        ],
        compiler_params=pltpu.CompilerParams(
            collective_id=0, has_side_effects=True, vmem_limit_bytes=60 * 1024 * 1024
        ),
        cost_estimate=pl.CostEstimate(
            flops=4 * cands * width * HT * TILE, bytes_accessed=5 * 2**20, transcendentals=0
        ),
    )(candidates, kv_cache, tile_owner, tile_slot, tile_length, norm_gain[None])


def solution(mesh):
    placed = (
        P(("groups", "cache", "req"), None, None, "rep"),
        P(("groups", "cache", "req"), None, None, "rep"),
        P(("groups", "cache", "req"), None),
        P(("groups", "cache", "req"), None),
        P(("groups", "cache", "req"), None),
        P("rep"),
    )
    return jax.shard_map(
        local,
        mesh=mesh,
        in_specs=placed,
        out_specs=P(("groups", "cache", "req"), None, "rep"),
        check_vma=False,
    )
```

```python
import functools
import math

import jax
import jax.numpy as jnp
from jax import lax
from jax.experimental import pallas as pl
from jax.experimental.pallas import tpu as pltpu
from jax.sharding import PartitionSpec as P

D = 1024
HEADS = 8
HEAD = D // HEADS
TILE = 64
HT = 16
HALF_SCALE = 0.5 / math.sqrt(HEAD)
ROWS = 128


def silu_half(half):
    return half + half * jnp.tanh(half)


def kernel(
    n, depth, split, cand_hbm, kv_hbm, owner_hbm, slot_hbm, length_hbm, gain_hbm, out_ref,
    cand_ref, kv_ref, lists, gain_ref,
    act, total, stats, peer_stats, table, wanted, wanted_s, own_tiles, outgoing, arrived,
    peer_query, peer_total, partial_out, partial_in, low_arrived,
    load_sem, list_send, list_recv, table_sem, tile_send, tile_recv, stat_send, stat_recv,
    query_send, query_recv, partial_send, partial_recv, low_send, low_recv,
):
    me = lax.axis_index("cache")
    core = lax.axis_index("rep")
    cands, width = total.shape
    peers = [lax.rem(me + d, n) for d in range(1, n)]
    middle = (me + 1) // 2 == 1
    edge = (me + 1) // 2 != 1
    near = 4 - 2 * me
    facing = 2 * (me // 3)
    half_width = width // 2

    list_loads = [
        pltpu.make_async_copy(src, lists.at[i], load_sem.at[i])
        for i, src in enumerate((owner_hbm, slot_hbm, length_hbm))
    ]
    cand_load = pltpu.make_async_copy(cand_hbm.at[0], cand_ref, load_sem.at[3])
    kv_load = pltpu.make_async_copy(kv_hbm, kv_ref, load_sem.at[4])
    gain_load = pltpu.make_async_copy(gain_hbm, gain_ref, load_sem.at[5])
    for load in list_loads + [cand_load, kv_load, gain_load]:
        load.start()

    barrier = pltpu.get_barrier_semaphore()
    for peer in peers:
        pl.semaphore_signal(
            barrier, inc=1, device_id={"cache": peer}, device_id_type=pl.DeviceIdType.MESH
        )
    pl.semaphore_signal(
        barrier, inc=1, device_id={"rep": 1 - core}, device_id_type=pl.DeviceIdType.MESH
    )
    for load in list_loads:
        load.wait()

    lane = lax.broadcasted_iota(jnp.int32, (n, 128), 1)
    row = lax.broadcasted_iota(jnp.int32, (n, 128), 0)

    def spread(i):
        padded = jnp.concatenate([lists[i], jnp.zeros((1, 128 - HT), jnp.int32)], axis=1)
        return jnp.broadcast_to(padded, (n, 128))

    owners, slots, lengths = spread(0), spread(1), spread(2)
    owned = ((owners == row) & (lengths > 0) & (lane < HT)).astype(jnp.int32)
    rank = owned
    for step in (1, 2, 4, 8):
        rank = rank + jnp.where(lane >= step, pltpu.roll(rank, step, 1), 0)
    slot_table = jnp.zeros((n, 128), jnp.int32)
    length_table = jnp.zeros((n, 128), jnp.int32)
    for k in range(depth):
        chosen = (owned > 0) & (rank == k + 1)
        slot_k = jnp.sum(jnp.where(chosen, slots, 0), axis=1, keepdims=True)
        length_k = jnp.sum(jnp.where(chosen, lengths, 0), axis=1, keepdims=True)
        slot_table = jnp.where(lane == k, slot_k, slot_table)
        length_table = jnp.where(lane == k, length_k, length_table)
    line = lax.broadcasted_iota(jnp.int32, (8, 128), 0)
    for o in range(n):
        table[o] = jnp.where(line == 0, slot_table[o : o + 1], length_table[o : o + 1])

    pl.semaphore_wait(barrier, n)
    list_copies = []
    for d, peer in enumerate(peers):
        copy = pltpu.make_async_remote_copy(
            src_ref=table,
            dst_ref=wanted.at[d],
            send_sem=list_send.at[d],
            recv_sem=list_recv.at[d],
            device_id={"cache": peer},
            device_id_type=pl.DeviceIdType.MESH,
        )
        copy.start()
        list_copies.append(copy)
    own_scalar = pltpu.make_async_copy(table.at[me], wanted_s.at[n - 1], table_sem.at[n - 1])
    own_scalar.start()

    def activate(parts):
        def one(block, carry):
            rows = pl.ds(pl.multiple_of(block * ROWS, ROWS), ROWS)
            for i in parts:
                half = cand_ref[rows, i, :].astype(jnp.float32) * 0.5
                act[i, rows, :] = silu_half(half).astype(jnp.bfloat16)
            return carry

        lax.fori_loop(0, cands // ROWS, one, 0)

    cand_load.wait()
    def to_partner(src, dst, send_sem, recv_sem):
        return pltpu.make_async_remote_copy(
            src_ref=src,
            dst_ref=dst,
            send_sem=send_sem,
            recv_sem=recv_sem,
            device_id={"cache": lax.rem(n + 3 - me, n)},
            device_id_type=pl.DeviceIdType.MESH,
        )

    def query_copy(cols):
        return to_partner(act.at[0, :, cols], peer_query.at[:, cols], query_send, query_recv)

    def partial_copy(cols):
        return to_partner(
            partial_out.at[:, cols], partial_in.at[:, cols], partial_send, partial_recv
        )

    every, low, high = slice(0, width), slice(0, half_width), slice(half_width, width)
    if split:
        activate((0,))
        pl.when(middle)(query_copy(every).start)
        pl.when(edge)(query_copy(low).start)

    to_scalar = []
    for d, copy in enumerate(list_copies):
        copy.wait_recv()
        move = pltpu.make_async_copy(wanted.at[d, me], wanted_s.at[d], table_sem.at[d])
        move.start()
        to_scalar.append(move)
    kv_load.wait()
    for move in to_scalar:
        move.wait()
    own_scalar.wait()

    def tile_copy(k, d, cols=every):
        to = lax.rem(me + n - d - 1, n)
        if split and d == 1:
            to = jnp.where(edge, 1 + me // 2, to)
        return pltpu.make_async_remote_copy(
            src_ref=outgoing.at[k, d, :, :, cols],
            dst_ref=arrived.at[k, d, :, :, cols],
            send_sem=tile_send.at[k, d],
            recv_sem=tile_recv.at[k, d],
            device_id={"cache": to},
            device_id_type=pl.DeviceIdType.MESH,
        )

    def low_copy(k):
        return pltpu.make_async_remote_copy(
            src_ref=outgoing.at[k, 1, :, :, low],
            dst_ref=low_arrived.at[k],
            send_sem=low_send.at[k],
            recv_sem=low_recv.at[k],
            device_id={"cache": jnp.where(me == 1, 0, n - 1)},
            device_id_type=pl.DeviceIdType.MESH,
        )

    def push(k, d, cols=every):
        outgoing[k, d] = kv_ref[wanted_s[d, 0, k]]
        tile_copy(k, d, cols).start()

    def push_low(k):
        outgoing[k, 1] = kv_ref[wanted_s[1, 0, k]]
        low_copy(k).start()

    def sends(d, action):
        if d == 1:
            pl.when(edge)(functools.partial(action, 1, every))
            pl.when(middle)(functools.partial(action, 1, high))
        else:
            pl.when(jnp.logical_and(middle, near != d))(functools.partial(action, d, every))
            pl.when(jnp.logical_and(edge, facing != d))(functools.partial(action, d, every))
            pl.when(jnp.logical_and(edge, facing == d))(functools.partial(action, d, high))

    if split:

        @pl.when(middle)
        def _():
            for k in range(depth):
                push_low(k)
            for k in range(depth):
                tile_copy(k, 1, high).start()

        @pl.when(edge)
        def _():
            for k in range(depth):
                push(k, 1)

        for k in range(depth):
            for d in (0, 2):
                sends(d, lambda d, cols, k=k: push(k, d, cols))
    else:
        for k in range(depth):
            for d in range(n - 1):
                push(k, d)

    activate((1, 2, 3) if split else (0, 1, 2, 3))

    def own_term(block, carry):
        rows = pl.ds(pl.multiple_of(block * ROWS, ROWS), ROWS)
        for h in range(width // HEAD):
            cols = slice(h * HEAD, (h + 1) * HEAD)
            query = act[0, rows, cols].astype(jnp.float32)
            key = act[1, rows, cols].astype(jnp.float32)
            value = act[2, rows, cols].astype(jnp.float32)
            score = jnp.sum(query * key, axis=1, keepdims=True)
            total[rows, cols] = silu_half(score * HALF_SCALE) * value
        return carry

    lax.fori_loop(0, cands // ROWS, own_term, 0)
    position = lax.broadcasted_iota(jnp.int32, (TILE, width), 0)

    def attend(query, result, tiles, counts, first=False, heads=None, clean=True):
        tile_count = len(counts)
        heads = range(width // HEAD) if heads is None else heads
        span = slice(0, width if len(heads) * HEAD == width else half_width)
        if heads[0] > 0:
            span = high
        for t in range(tile_count if clean else 0):
            live = (position[:, span] < counts[t]).astype(jnp.float32)
            tiles[t, 0, :, span] = (
                tiles[t, 0, :, span].astype(jnp.float32) * live
            ).astype(jnp.bfloat16)

        def one(block, carry):
            rows = pl.ds(pl.multiple_of(block * ROWS, ROWS), ROWS)
            for h in heads:
                cols = slice(h * HEAD, (h + 1) * HEAD)
                keys = tiles[:, 0, :, cols].reshape(tile_count * TILE, HEAD)
                values = tiles[:, 1, :, cols].reshape(tile_count * TILE, HEAD)
                scores = lax.dot_general(
                    query[rows, cols], keys, (((1,), (1,)), ((), ())),
                    preferred_element_type=jnp.float32,
                )
                weights = silu_half(scores * HALF_SCALE).astype(jnp.bfloat16)
                added = jnp.dot(weights, values, preferred_element_type=jnp.float32)
                result[rows, cols] = added if first else result[rows, cols] + added
            return carry

        lax.fori_loop(0, cands // ROWS, one, 0)

    def counts_of(ref):
        block = ref[...]
        return [block[1:2, k : k + 1] for k in range(depth)]

    for k in range(depth):
        own_tiles[k] = kv_ref[wanted_s[n - 1, 0, k]]
    attend(act.at[0], total, own_tiles, counts_of(table.at[me]))

    def from_all():
        for k in range(depth):
            counts = []
            for d in range(n - 1):
                tile_copy(k, d).wait_recv()
                counts.append(table[lax.rem(me + d + 1, n)][1:2, k : k + 1])
            attend(act.at[0], total, arrived.at[k], counts)

    def serve(mine, tiles, side, slot, cols, heads):
        for k in range(depth):
            own_tiles[k] = kv_ref[wanted_s[slot, 0, k]]
        query_copy(cols).wait_recv()
        attend(peer_query, peer_total, own_tiles, counts_of(mine), first=True, heads=heads)
        for k in range(depth):
            if cols is every:
                tile_copy(k, 1).wait_recv()
            else:
                low_copy(k).wait_recv()
        attend(peer_query, peer_total, tiles, counts_of(wanted.at[slot, side]), heads=heads)

        def narrow(block, carry):
            rows = pl.ds(pl.multiple_of(block * ROWS, ROWS), ROWS)
            partial_out[rows, cols] = peer_total[rows, cols].astype(jnp.bfloat16)
            return carry

        lax.fori_loop(0, cands // ROWS, narrow, 0)
        partial_copy(cols).start()

    def collect(cols):
        partial_copy(cols).wait_recv()

        def widen(block, carry):
            rows = pl.ds(pl.multiple_of(block * ROWS, ROWS), ROWS)
            total[rows, cols] += partial_in[rows, cols].astype(jnp.float32)
            return carry

        lax.fori_loop(0, cands // ROWS, widen, 0)

    def at_middle():
        side = 3 * (me - 1)
        serve(wanted.at[near, me], arrived.at[:, 1], side, near, every, None)
        for d in (0, 2):

            @pl.when(near == d)
            def _():
                for k in range(depth):
                    tile_copy(k, d).wait_recv()
                attend(act.at[0], total, arrived.at[:, d], counts_of(table.at[side]))

        collect(every)

    def at_edge():
        side = 1 + me // 3
        lows, highs = (0, 1), (2, 3)
        serve(wanted.at[facing, me], low_arrived, side, facing, low, lows)
        for k in range(depth):
            counts = []
            for d in range(n - 1):
                if d == 1:
                    tile_copy(k, d, high).wait_recv()
                else:
                    pl.when(facing == d)(tile_copy(k, d).wait_recv)
                    pl.when(facing != d)(tile_copy(k, d, high).wait_recv)
                counts.append(table[lax.rem(me + d + 1, n)][1:2, k : k + 1])
            attend(act.at[0], total, arrived.at[k], counts, heads=highs)
            for d in (0, 2):

                @pl.when(facing == d)
                def _():
                    attend(
                        act.at[0], total, arrived.at[k, d : d + 1], counts[d : d + 1], heads=lows
                    )

        collect(low)

    if split:
        pl.when(edge)(at_edge)
        pl.when(middle)(at_middle)
    else:
        from_all()

    gain_load.wait()

    def moments(block, carry):
        rows = pl.ds(pl.multiple_of(block * ROWS, ROWS), ROWS)
        attended = total[rows, :] * (1.0 / (HT * TILE + 1))
        sums = jnp.sum(attended, axis=1, keepdims=True)
        squares = jnp.sum(attended * attended, axis=1, keepdims=True)
        at = lax.broadcasted_iota(jnp.int32, (ROWS, 128), 1)
        stats[rows, :] = jnp.where(at < 64, sums, squares)
        return carry

    lax.fori_loop(0, cands // ROWS, moments, 0)
    stat_copy = pltpu.make_async_remote_copy(
        src_ref=stats,
        dst_ref=peer_stats,
        send_sem=stat_send,
        recv_sem=stat_recv,
        device_id={"rep": 1 - core},
        device_id_type=pl.DeviceIdType.MESH,
    )
    stat_copy.start()
    stat_copy.wait_recv()

    def finish(block, carry):
        rows = pl.ds(pl.multiple_of(block * ROWS, ROWS), ROWS)
        both = stats[rows, :] + peer_stats[rows, :]
        average = both[:, 0:1] * (1.0 / D)
        variance = both[:, 64:65] * (1.0 / D) - average * average
        attended = total[rows, :] * (1.0 / (HT * TILE + 1))
        normed = (attended - average) * lax.rsqrt(variance + 1e-05) * gain_ref[...]
        out_ref[0, rows, :] = (normed * act[3, rows, :].astype(jnp.float32)).astype(jnp.bfloat16)
        return carry

    lax.fori_loop(0, cands // ROWS, finish, 0)
    stat_copy.wait_send()
    for copy in list_copies:
        copy.wait_send()
    if split:
        for k in range(depth):
            for d in range(n - 1):
                sends(d, lambda d, cols, k=k: tile_copy(k, d, cols).wait_send())

        @pl.when(middle)
        def _():
            for k in range(depth):
                low_copy(k).wait_send()
            query_copy(every).wait_send()
            partial_copy(every).wait_send()

        @pl.when(edge)
        def _():
            query_copy(low).wait_send()
            partial_copy(low).wait_send()
    else:
        for k in range(depth):
            for d in range(n - 1):
                tile_copy(k, d).wait_send()


def local(candidates, kv_cache, tile_owner, tile_slot, tile_length, norm_gain):
    n = lax.axis_size("cache")
    depth = (HT - 2) // n + 2
    cands, width = candidates.shape[1], candidates.shape[3]
    vmem = pl.BlockSpec(memory_space=pltpu.VMEM)
    tile = (2, TILE, width)
    dma = pltpu.SemaphoreType.DMA
    return pl.pallas_call(
        functools.partial(kernel, n, depth, n == 4),
        out_shape=jax.ShapeDtypeStruct((1, cands, width), jnp.bfloat16),
        in_specs=[pl.BlockSpec(memory_space=pltpu.HBM)] * 6,
        out_specs=vmem,
        scratch_shapes=[
            pltpu.VMEM((cands, 4, width), jnp.bfloat16),
            pltpu.VMEM(kv_cache.shape, jnp.bfloat16),
            pltpu.VMEM((3, 1, HT), jnp.int32),
            pltpu.VMEM((1, width), jnp.float32),
            pltpu.VMEM((4, cands, width), jnp.bfloat16),
            pltpu.VMEM((cands, width), jnp.float32),
            pltpu.VMEM((cands, 128), jnp.float32),
            pltpu.VMEM((cands, 128), jnp.float32),
            pltpu.VMEM((n, 8, 128), jnp.int32),
            pltpu.VMEM((n - 1, n, 8, 128), jnp.int32),
            pltpu.SMEM((n, 8, 128), jnp.int32),
            pltpu.VMEM((depth,) + tile, jnp.bfloat16),
            pltpu.VMEM((depth, n - 1) + tile, jnp.bfloat16),
            pltpu.VMEM((depth, n - 1) + tile, jnp.bfloat16),
            pltpu.VMEM((cands, width), jnp.bfloat16),
            pltpu.VMEM((cands, width), jnp.float32),
            pltpu.VMEM((cands, width), jnp.bfloat16),
            pltpu.VMEM((cands, width), jnp.bfloat16),
            pltpu.VMEM((depth, 2, TILE, width // 2), jnp.bfloat16),
            dma((6,)),
            dma((n - 1,)),
            dma((n - 1,)),
            dma((n,)),
            dma((depth, n - 1)),
            dma((depth, n - 1)),
            dma,
            dma,
            dma,
            dma,
            dma,
            dma,
            dma((depth,)),
            dma((depth,)),
        ],
        compiler_params=pltpu.CompilerParams(
            collective_id=0, has_side_effects=True, vmem_limit_bytes=60 * 1024 * 1024
        ),
        cost_estimate=pl.CostEstimate(
            flops=4 * cands * width * HT * TILE, bytes_accessed=5 * 2**20, transcendentals=0
        ),
    )(candidates, kv_cache, tile_owner, tile_slot, tile_length, norm_gain[None])


def solution(mesh):
    placed = (
        P(("groups", "cache", "req"), None, None, "rep"),
        P(("groups", "cache", "req"), None, None, "rep"),
        P(("groups", "cache", "req"), None),
        P(("groups", "cache", "req"), None),
        P(("groups", "cache", "req"), None),
        P("rep"),
    )
    return jax.shard_map(
        local,
        mesh=mesh,
        in_specs=placed,
        out_specs=P(("groups", "cache", "req"), None, "rep"),
        check_vma=False,
    )
```

```python
import functools
import math

import jax
import jax.numpy as jnp
from jax import lax
from jax.experimental import pallas as pl
from jax.experimental.pallas import tpu as pltpu
from jax.sharding import PartitionSpec as P

D = 1024
HEADS = 8
HEAD = D // HEADS
TILE = 64
HT = 16
HALF_SCALE = 0.5 / math.sqrt(HEAD)
ROWS = 128


def silu_half(half):
    return half + half * jnp.tanh(half)


def kernel(
    n, depth, split, cand_hbm, kv_hbm, owner_hbm, slot_hbm, length_hbm, gain_hbm, out_ref,
    cand_ref, kv_ref, lists, gain_ref,
    act, total, stats, peer_stats, table, wanted, wanted_s, own_tiles, outgoing, arrived,
    peer_query, peer_total, partial_out, partial_in, low_arrived,
    load_sem, list_send, list_recv, table_sem, tile_send, tile_recv, stat_send, stat_recv,
    query_send, query_recv, partial_send, partial_recv, low_send, low_recv,
):
    me = lax.axis_index("cache")
    core = lax.axis_index("rep")
    cands, width = total.shape
    peers = [lax.rem(me + d, n) for d in range(1, n)]
    middle = (me + 1) // 2 == 1
    edge = (me + 1) // 2 != 1
    near = 4 - 2 * me
    facing = 2 * (me // 3)
    half_width = width // 2

    list_loads = [
        pltpu.make_async_copy(src, lists.at[i], load_sem.at[i])
        for i, src in enumerate((owner_hbm, slot_hbm, length_hbm))
    ]
    cand_load = pltpu.make_async_copy(cand_hbm.at[0], cand_ref, load_sem.at[3])
    kv_load = pltpu.make_async_copy(kv_hbm, kv_ref, load_sem.at[4])
    gain_load = pltpu.make_async_copy(gain_hbm, gain_ref, load_sem.at[5])
    for load in list_loads + [cand_load, kv_load, gain_load]:
        load.start()

    barrier = pltpu.get_barrier_semaphore()
    for peer in peers:
        pl.semaphore_signal(
            barrier, inc=1, device_id={"cache": peer}, device_id_type=pl.DeviceIdType.MESH
        )
    pl.semaphore_signal(
        barrier, inc=1, device_id={"rep": 1 - core}, device_id_type=pl.DeviceIdType.MESH
    )
    for load in list_loads:
        load.wait()

    lane = lax.broadcasted_iota(jnp.int32, (n, 128), 1)
    row = lax.broadcasted_iota(jnp.int32, (n, 128), 0)

    def spread(i):
        padded = jnp.concatenate([lists[i], jnp.zeros((1, 128 - HT), jnp.int32)], axis=1)
        return jnp.broadcast_to(padded, (n, 128))

    owners, slots, lengths = spread(0), spread(1), spread(2)
    owned = ((owners == row) & (lengths > 0) & (lane < HT)).astype(jnp.int32)
    rank = owned
    for step in (1, 2, 4, 8):
        rank = rank + jnp.where(lane >= step, pltpu.roll(rank, step, 1), 0)
    slot_table = jnp.zeros((n, 128), jnp.int32)
    length_table = jnp.zeros((n, 128), jnp.int32)
    for k in range(depth):
        chosen = (owned > 0) & (rank == k + 1)
        slot_k = jnp.sum(jnp.where(chosen, slots, 0), axis=1, keepdims=True)
        length_k = jnp.sum(jnp.where(chosen, lengths, 0), axis=1, keepdims=True)
        slot_table = jnp.where(lane == k, slot_k, slot_table)
        length_table = jnp.where(lane == k, length_k, length_table)
    line = lax.broadcasted_iota(jnp.int32, (8, 128), 0)
    for o in range(n):
        table[o] = jnp.where(line == 0, slot_table[o : o + 1], length_table[o : o + 1])

    pl.semaphore_wait(barrier, n)
    list_copies = []
    for d, peer in enumerate(peers):
        copy = pltpu.make_async_remote_copy(
            src_ref=table,
            dst_ref=wanted.at[d],
            send_sem=list_send.at[d],
            recv_sem=list_recv.at[d],
            device_id={"cache": peer},
            device_id_type=pl.DeviceIdType.MESH,
        )
        copy.start()
        list_copies.append(copy)
    own_scalar = pltpu.make_async_copy(table.at[me], wanted_s.at[n - 1], table_sem.at[n - 1])
    own_scalar.start()

    def activate(parts):
        def one(block, carry):
            rows = pl.ds(pl.multiple_of(block * ROWS, ROWS), ROWS)
            for i in parts:
                half = cand_ref[rows, i, :].astype(jnp.float32) * 0.5
                act[i, rows, :] = silu_half(half).astype(jnp.bfloat16)
            return carry

        lax.fori_loop(0, cands // ROWS, one, 0)

    cand_load.wait()
    def to_partner(src, dst, send_sem, recv_sem):
        return pltpu.make_async_remote_copy(
            src_ref=src,
            dst_ref=dst,
            send_sem=send_sem,
            recv_sem=recv_sem,
            device_id={"cache": lax.rem(n + 3 - me, n)},
            device_id_type=pl.DeviceIdType.MESH,
        )

    def query_copy(cols):
        return to_partner(act.at[0, :, cols], peer_query.at[:, cols], query_send, query_recv)

    def partial_copy(cols):
        return to_partner(
            partial_out.at[:, cols], partial_in.at[:, cols], partial_send, partial_recv
        )

    every, low, high = slice(0, width), slice(0, half_width), slice(half_width, width)
    if split:
        activate((0,))
        pl.when(middle)(query_copy(every).start)
        pl.when(edge)(query_copy(low).start)

    to_scalar = []
    for d, copy in enumerate(list_copies):
        copy.wait_recv()
        move = pltpu.make_async_copy(wanted.at[d, me], wanted_s.at[d], table_sem.at[d])
        move.start()
        to_scalar.append(move)
    kv_load.wait()
    for move in to_scalar:
        move.wait()
    own_scalar.wait()

    def tile_copy(k, d, cols=every):
        to = lax.rem(me + n - d - 1, n)
        if split and d == 1:
            to = jnp.where(edge, 1 + me // 2, to)
        return pltpu.make_async_remote_copy(
            src_ref=outgoing.at[k, d, :, :, cols],
            dst_ref=arrived.at[k, d, :, :, cols],
            send_sem=tile_send.at[k, d],
            recv_sem=tile_recv.at[k, d],
            device_id={"cache": to},
            device_id_type=pl.DeviceIdType.MESH,
        )

    def low_copy(k):
        return pltpu.make_async_remote_copy(
            src_ref=outgoing.at[k, 1, :, :, low],
            dst_ref=low_arrived.at[k],
            send_sem=low_send.at[k],
            recv_sem=low_recv.at[k],
            device_id={"cache": jnp.where(me == 1, 0, n - 1)},
            device_id_type=pl.DeviceIdType.MESH,
        )

    def push(k, d, cols=every):
        outgoing[k, d] = kv_ref[wanted_s[d, 0, k]]
        tile_copy(k, d, cols).start()

    def push_low(k):
        outgoing[k, 1] = kv_ref[wanted_s[1, 0, k]]
        low_copy(k).start()

    def sends(d, action):
        if d == 1:
            pl.when(edge)(functools.partial(action, 1, every))
            pl.when(middle)(functools.partial(action, 1, high))
        else:
            pl.when(jnp.logical_and(middle, near != d))(functools.partial(action, d, every))
            pl.when(jnp.logical_and(edge, facing != d))(functools.partial(action, d, every))
            pl.when(jnp.logical_and(edge, facing == d))(functools.partial(action, d, high))

    if split:

        @pl.when(middle)
        def _():
            for k in range(depth):
                push_low(k)
            for k in range(depth):
                tile_copy(k, 1, high).start()

        @pl.when(edge)
        def _():
            for k in range(depth):
                push(k, 1)

        for k in range(depth):
            for d in (0, 2):
                far = jnp.logical_and(edge, facing == d)
                pl.when(far)(functools.partial(push, k, d, high))
        for k in range(depth):
            for d in (0, 2):
                close = jnp.where(edge, facing != d, near != d)
                pl.when(close)(functools.partial(push, k, d))
    else:
        for k in range(depth):
            for d in range(n - 1):
                push(k, d)

    activate((1, 2, 3) if split else (0, 1, 2, 3))

    def own_term(block, carry):
        rows = pl.ds(pl.multiple_of(block * ROWS, ROWS), ROWS)
        for h in range(width // HEAD):
            cols = slice(h * HEAD, (h + 1) * HEAD)
            query = act[0, rows, cols].astype(jnp.float32)
            key = act[1, rows, cols].astype(jnp.float32)
            value = act[2, rows, cols].astype(jnp.float32)
            score = jnp.sum(query * key, axis=1, keepdims=True)
            total[rows, cols] = silu_half(score * HALF_SCALE) * value
        return carry

    lax.fori_loop(0, cands // ROWS, own_term, 0)
    position = lax.broadcasted_iota(jnp.int32, (TILE, width), 0)

    def attend(query, result, tiles, counts, first=False, heads=None, clean=True):
        tile_count = len(counts)
        heads = range(width // HEAD) if heads is None else heads
        span = slice(0, width if len(heads) * HEAD == width else half_width)
        if heads[0] > 0:
            span = high
        for t in range(tile_count if clean else 0):
            live = (position[:, span] < counts[t]).astype(jnp.float32)
            tiles[t, 0, :, span] = (
                tiles[t, 0, :, span].astype(jnp.float32) * live
            ).astype(jnp.bfloat16)

        def one(block, carry):
            rows = pl.ds(pl.multiple_of(block * ROWS, ROWS), ROWS)
            for h in heads:
                cols = slice(h * HEAD, (h + 1) * HEAD)
                keys = tiles[:, 0, :, cols].reshape(tile_count * TILE, HEAD)
                values = tiles[:, 1, :, cols].reshape(tile_count * TILE, HEAD)
                scores = lax.dot_general(
                    query[rows, cols], keys, (((1,), (1,)), ((), ())),
                    preferred_element_type=jnp.float32,
                )
                weights = silu_half(scores * HALF_SCALE).astype(jnp.bfloat16)
                added = jnp.dot(weights, values, preferred_element_type=jnp.float32)
                result[rows, cols] = added if first else result[rows, cols] + added
            return carry

        lax.fori_loop(0, cands // ROWS, one, 0)

    def counts_of(ref):
        block = ref[...]
        return [block[1:2, k : k + 1] for k in range(depth)]

    for k in range(depth):
        own_tiles[k] = kv_ref[wanted_s[n - 1, 0, k]]
    attend(act.at[0], total, own_tiles, counts_of(table.at[me]))

    def from_all():
        for k in range(depth):
            counts = []
            for d in range(n - 1):
                tile_copy(k, d).wait_recv()
                counts.append(table[lax.rem(me + d + 1, n)][1:2, k : k + 1])
            attend(act.at[0], total, arrived.at[k], counts)

    def serve(mine, tiles, side, slot, cols, heads):
        for k in range(depth):
            own_tiles[k] = kv_ref[wanted_s[slot, 0, k]]
        query_copy(cols).wait_recv()
        attend(peer_query, peer_total, own_tiles, counts_of(mine), first=True, heads=heads)
        for k in range(depth):
            if cols is every:
                tile_copy(k, 1).wait_recv()
            else:
                low_copy(k).wait_recv()
        attend(peer_query, peer_total, tiles, counts_of(wanted.at[slot, side]), heads=heads)

        def narrow(block, carry):
            rows = pl.ds(pl.multiple_of(block * ROWS, ROWS), ROWS)
            partial_out[rows, cols] = peer_total[rows, cols].astype(jnp.bfloat16)
            return carry

        lax.fori_loop(0, cands // ROWS, narrow, 0)
        partial_copy(cols).start()

    def collect(cols):
        partial_copy(cols).wait_recv()

        def widen(block, carry):
            rows = pl.ds(pl.multiple_of(block * ROWS, ROWS), ROWS)
            total[rows, cols] += partial_in[rows, cols].astype(jnp.float32)
            return carry

        lax.fori_loop(0, cands // ROWS, widen, 0)

    def at_middle():
        side = 3 * (me - 1)
        serve(wanted.at[near, me], arrived.at[:, 1], side, near, every, None)
        for d in (0, 2):

            @pl.when(near == d)
            def _():
                for k in range(depth):
                    tile_copy(k, d).wait_recv()
                attend(act.at[0], total, arrived.at[:, d], counts_of(table.at[side]))

        collect(every)

    def at_edge():
        side = 1 + me // 3
        lows, highs = (0, 1), (2, 3)
        serve(wanted.at[facing, me], low_arrived, side, facing, low, lows)
        for k in range(depth):
            counts = []
            for d in range(n - 1):
                if d == 1:
                    tile_copy(k, d, high).wait_recv()
                else:
                    pl.when(facing == d)(tile_copy(k, d).wait_recv)
                    pl.when(facing != d)(tile_copy(k, d, high).wait_recv)
                counts.append(table[lax.rem(me + d + 1, n)][1:2, k : k + 1])
            attend(act.at[0], total, arrived.at[k], counts, heads=highs)
            for d in (0, 2):

                @pl.when(facing == d)
                def _():
                    attend(
                        act.at[0], total, arrived.at[k, d : d + 1], counts[d : d + 1], heads=lows
                    )

        collect(low)

    if split:
        pl.when(edge)(at_edge)
        pl.when(middle)(at_middle)
    else:
        from_all()

    gain_load.wait()

    def moments(block, carry):
        rows = pl.ds(pl.multiple_of(block * ROWS, ROWS), ROWS)
        attended = total[rows, :] * (1.0 / (HT * TILE + 1))
        sums = jnp.sum(attended, axis=1, keepdims=True)
        squares = jnp.sum(attended * attended, axis=1, keepdims=True)
        at = lax.broadcasted_iota(jnp.int32, (ROWS, 128), 1)
        stats[rows, :] = jnp.where(at < 64, sums, squares)
        return carry

    lax.fori_loop(0, cands // ROWS, moments, 0)
    stat_copy = pltpu.make_async_remote_copy(
        src_ref=stats,
        dst_ref=peer_stats,
        send_sem=stat_send,
        recv_sem=stat_recv,
        device_id={"rep": 1 - core},
        device_id_type=pl.DeviceIdType.MESH,
    )
    stat_copy.start()
    stat_copy.wait_recv()

    def finish(block, carry):
        rows = pl.ds(pl.multiple_of(block * ROWS, ROWS), ROWS)
        both = stats[rows, :] + peer_stats[rows, :]
        average = both[:, 0:1] * (1.0 / D)
        variance = both[:, 64:65] * (1.0 / D) - average * average
        attended = total[rows, :] * (1.0 / (HT * TILE + 1))
        normed = (attended - average) * lax.rsqrt(variance + 1e-05) * gain_ref[...]
        out_ref[0, rows, :] = (normed * act[3, rows, :].astype(jnp.float32)).astype(jnp.bfloat16)
        return carry

    lax.fori_loop(0, cands // ROWS, finish, 0)
    stat_copy.wait_send()
    for copy in list_copies:
        copy.wait_send()
    if split:
        for k in range(depth):
            for d in range(n - 1):
                sends(d, lambda d, cols, k=k: tile_copy(k, d, cols).wait_send())

        @pl.when(middle)
        def _():
            for k in range(depth):
                low_copy(k).wait_send()
            query_copy(every).wait_send()
            partial_copy(every).wait_send()

        @pl.when(edge)
        def _():
            query_copy(low).wait_send()
            partial_copy(low).wait_send()
    else:
        for k in range(depth):
            for d in range(n - 1):
                tile_copy(k, d).wait_send()


def local(candidates, kv_cache, tile_owner, tile_slot, tile_length, norm_gain):
    n = lax.axis_size("cache")
    depth = (HT - 2) // n + 2
    cands, width = candidates.shape[1], candidates.shape[3]
    vmem = pl.BlockSpec(memory_space=pltpu.VMEM)
    tile = (2, TILE, width)
    dma = pltpu.SemaphoreType.DMA
    return pl.pallas_call(
        functools.partial(kernel, n, depth, n == 4),
        out_shape=jax.ShapeDtypeStruct((1, cands, width), jnp.bfloat16),
        in_specs=[pl.BlockSpec(memory_space=pltpu.HBM)] * 6,
        out_specs=vmem,
        scratch_shapes=[
            pltpu.VMEM((cands, 4, width), jnp.bfloat16),
            pltpu.VMEM(kv_cache.shape, jnp.bfloat16),
            pltpu.VMEM((3, 1, HT), jnp.int32),
            pltpu.VMEM((1, width), jnp.float32),
            pltpu.VMEM((4, cands, width), jnp.bfloat16),
            pltpu.VMEM((cands, width), jnp.float32),
            pltpu.VMEM((cands, 128), jnp.float32),
            pltpu.VMEM((cands, 128), jnp.float32),
            pltpu.VMEM((n, 8, 128), jnp.int32),
            pltpu.VMEM((n - 1, n, 8, 128), jnp.int32),
            pltpu.SMEM((n, 8, 128), jnp.int32),
            pltpu.VMEM((depth,) + tile, jnp.bfloat16),
            pltpu.VMEM((depth, n - 1) + tile, jnp.bfloat16),
            pltpu.VMEM((depth, n - 1) + tile, jnp.bfloat16),
            pltpu.VMEM((cands, width), jnp.bfloat16),
            pltpu.VMEM((cands, width), jnp.float32),
            pltpu.VMEM((cands, width), jnp.bfloat16),
            pltpu.VMEM((cands, width), jnp.bfloat16),
            pltpu.VMEM((depth, 2, TILE, width // 2), jnp.bfloat16),
            dma((6,)),
            dma((n - 1,)),
            dma((n - 1,)),
            dma((n,)),
            dma((depth, n - 1)),
            dma((depth, n - 1)),
            dma,
            dma,
            dma,
            dma,
            dma,
            dma,
            dma((depth,)),
            dma((depth,)),
        ],
        compiler_params=pltpu.CompilerParams(
            collective_id=0, has_side_effects=True, vmem_limit_bytes=60 * 1024 * 1024
        ),
        cost_estimate=pl.CostEstimate(
            flops=4 * cands * width * HT * TILE, bytes_accessed=5 * 2**20, transcendentals=0
        ),
    )(candidates, kv_cache, tile_owner, tile_slot, tile_length, norm_gain[None])


def solution(mesh):
    placed = (
        P(("groups", "cache", "req"), None, None, "rep"),
        P(("groups", "cache", "req"), None, None, "rep"),
        P(("groups", "cache", "req"), None),
        P(("groups", "cache", "req"), None),
        P(("groups", "cache", "req"), None),
        P("rep"),
    )
    return jax.shard_map(
        local,
        mesh=mesh,
        in_specs=placed,
        out_specs=P(("groups", "cache", "req"), None, "rep"),
        check_vma=False,
    )
```

```python
import functools
import math

import jax
import jax.numpy as jnp
from jax import lax
from jax.experimental import pallas as pl
from jax.experimental.pallas import tpu as pltpu
from jax.sharding import PartitionSpec as P

D = 1024
HEADS = 8
HEAD = D // HEADS
TILE = 64
HT = 16
HALF_SCALE = 0.5 / math.sqrt(HEAD)
ROWS = 128


def silu_half(half):
    return half + half * jnp.tanh(half)


def kernel(
    n, depth, split, cand_hbm, kv_hbm, owner_hbm, slot_hbm, length_hbm, gain_hbm, out_ref,
    cand_ref, kv_ref, lists, gain_ref,
    act, total, stats, peer_stats, table, wanted, wanted_s, own_tiles, outgoing, arrived,
    peer_query, peer_total, partial_out, partial_in, low_arrived,
    load_sem, list_send, list_recv, table_sem, tile_send, tile_recv, stat_send, stat_recv,
    query_send, query_recv, partial_send, partial_recv, low_send, low_recv,
):
    me = lax.axis_index("cache")
    core = lax.axis_index("rep")
    cands, width = total.shape
    peers = [lax.rem(me + d, n) for d in range(1, n)]
    middle = (me + 1) // 2 == 1
    edge = (me + 1) // 2 != 1
    near = 4 - 2 * me
    facing = 2 * (me // 3)
    half_width = width // 2

    list_loads = [
        pltpu.make_async_copy(src, lists.at[i], load_sem.at[i])
        for i, src in enumerate((owner_hbm, slot_hbm, length_hbm))
    ]
    cand_load = pltpu.make_async_copy(cand_hbm.at[0], cand_ref, load_sem.at[3])
    kv_load = pltpu.make_async_copy(kv_hbm, kv_ref, load_sem.at[4])
    gain_load = pltpu.make_async_copy(gain_hbm, gain_ref, load_sem.at[5])
    for load in list_loads + [cand_load, kv_load, gain_load]:
        load.start()

    barrier = pltpu.get_barrier_semaphore()
    for peer in peers:
        pl.semaphore_signal(
            barrier, inc=1, device_id={"cache": peer}, device_id_type=pl.DeviceIdType.MESH
        )
    pl.semaphore_signal(
        barrier, inc=1, device_id={"rep": 1 - core}, device_id_type=pl.DeviceIdType.MESH
    )
    for load in list_loads:
        load.wait()

    lane = lax.broadcasted_iota(jnp.int32, (n, 128), 1)
    row = lax.broadcasted_iota(jnp.int32, (n, 128), 0)

    def spread(i):
        padded = jnp.concatenate([lists[i], jnp.zeros((1, 128 - HT), jnp.int32)], axis=1)
        return jnp.broadcast_to(padded, (n, 128))

    owners, slots, lengths = spread(0), spread(1), spread(2)
    owned = ((owners == row) & (lengths > 0) & (lane < HT)).astype(jnp.int32)
    rank = owned
    for step in (1, 2, 4, 8):
        rank = rank + jnp.where(lane >= step, pltpu.roll(rank, step, 1), 0)
    slot_table = jnp.zeros((n, 128), jnp.int32)
    length_table = jnp.zeros((n, 128), jnp.int32)
    for k in range(depth):
        chosen = (owned > 0) & (rank == k + 1)
        slot_k = jnp.sum(jnp.where(chosen, slots, 0), axis=1, keepdims=True)
        length_k = jnp.sum(jnp.where(chosen, lengths, 0), axis=1, keepdims=True)
        slot_table = jnp.where(lane == k, slot_k, slot_table)
        length_table = jnp.where(lane == k, length_k, length_table)
    line = lax.broadcasted_iota(jnp.int32, (8, 128), 0)
    for o in range(n):
        table[o] = jnp.where(line == 0, slot_table[o : o + 1], length_table[o : o + 1])

    pl.semaphore_wait(barrier, n)
    list_copies = []
    for d, peer in enumerate(peers):
        copy = pltpu.make_async_remote_copy(
            src_ref=table,
            dst_ref=wanted.at[d],
            send_sem=list_send.at[d],
            recv_sem=list_recv.at[d],
            device_id={"cache": peer},
            device_id_type=pl.DeviceIdType.MESH,
        )
        copy.start()
        list_copies.append(copy)
    own_scalar = pltpu.make_async_copy(table.at[me], wanted_s.at[n - 1], table_sem.at[n - 1])
    own_scalar.start()

    def activate(parts):
        def one(block, carry):
            rows = pl.ds(pl.multiple_of(block * ROWS, ROWS), ROWS)
            for i in parts:
                half = cand_ref[rows, i, :].astype(jnp.float32) * 0.5
                act[i, rows, :] = silu_half(half).astype(jnp.bfloat16)
            return carry

        lax.fori_loop(0, cands // ROWS, one, 0)

    cand_load.wait()
    def to_partner(src, dst, send_sem, recv_sem):
        return pltpu.make_async_remote_copy(
            src_ref=src,
            dst_ref=dst,
            send_sem=send_sem,
            recv_sem=recv_sem,
            device_id={"cache": lax.rem(n + 3 - me, n)},
            device_id_type=pl.DeviceIdType.MESH,
        )

    def query_copy(cols):
        return to_partner(act.at[0, :, cols], peer_query.at[:, cols], query_send, query_recv)

    def partial_copy(cols):
        return to_partner(
            partial_out.at[:, cols], partial_in.at[:, cols], partial_send, partial_recv
        )

    every, low, high = slice(0, width), slice(0, half_width), slice(half_width, width)
    if split:
        activate((0,))
        pl.when(middle)(query_copy(every).start)
        pl.when(edge)(query_copy(low).start)

    to_scalar = []
    for d, copy in enumerate(list_copies):
        copy.wait_recv()
        move = pltpu.make_async_copy(wanted.at[d, me], wanted_s.at[d], table_sem.at[d])
        move.start()
        to_scalar.append(move)
    kv_load.wait()
    for move in to_scalar:
        move.wait()
    own_scalar.wait()

    def tile_copy(k, d, cols=every):
        to = lax.rem(me + n - d - 1, n)
        if split and d == 1:
            to = jnp.where(edge, 1 + me // 2, to)
        return pltpu.make_async_remote_copy(
            src_ref=outgoing.at[k, d, :, :, cols],
            dst_ref=arrived.at[k, d, :, :, cols],
            send_sem=tile_send.at[k, d],
            recv_sem=tile_recv.at[k, d],
            device_id={"cache": to},
            device_id_type=pl.DeviceIdType.MESH,
        )

    def low_copy(k):
        return pltpu.make_async_remote_copy(
            src_ref=outgoing.at[k, 1, :, :, low],
            dst_ref=low_arrived.at[k],
            send_sem=low_send.at[k],
            recv_sem=low_recv.at[k],
            device_id={"cache": jnp.where(me == 1, 0, n - 1)},
            device_id_type=pl.DeviceIdType.MESH,
        )

    def push(k, d, cols=every):
        outgoing[k, d] = kv_ref[wanted_s[d, 0, k]]
        tile_copy(k, d, cols).start()

    def push_low(k):
        outgoing[k, 1] = kv_ref[wanted_s[1, 0, k]]
        low_copy(k).start()

    def sends(d, action):
        if d == 1:
            pl.when(edge)(functools.partial(action, 1, every))
            pl.when(middle)(functools.partial(action, 1, high))
        else:
            pl.when(jnp.logical_and(middle, near != d))(functools.partial(action, d, every))
            pl.when(jnp.logical_and(edge, facing != d))(functools.partial(action, d, every))
            pl.when(jnp.logical_and(edge, facing == d))(functools.partial(action, d, high))

    if split:

        @pl.when(middle)
        def _():
            for k in range(depth):
                push_low(k)
                tile_copy(k, 1, high).start()
                for d in (0, 2):
                    pl.when(near != d)(functools.partial(push, k, d))

        @pl.when(edge)
        def _():
            for k in range(depth):
                push(k, 1)

        for k in range(depth):
            for d in (0, 2):
                pl.when(edge & (facing != d))(functools.partial(push, k, d))
                pl.when(edge & (facing == d))(functools.partial(push, k, d, high))
    else:
        for k in range(depth):
            for d in range(n - 1):
                push(k, d)

    activate((1, 2, 3) if split else (0, 1, 2, 3))

    def own_term(block, carry):
        rows = pl.ds(pl.multiple_of(block * ROWS, ROWS), ROWS)
        for h in range(width // HEAD):
            cols = slice(h * HEAD, (h + 1) * HEAD)
            query = act[0, rows, cols].astype(jnp.float32)
            key = act[1, rows, cols].astype(jnp.float32)
            value = act[2, rows, cols].astype(jnp.float32)
            score = jnp.sum(query * key, axis=1, keepdims=True)
            total[rows, cols] = silu_half(score * HALF_SCALE) * value
        return carry

    lax.fori_loop(0, cands // ROWS, own_term, 0)
    position = lax.broadcasted_iota(jnp.int32, (TILE, width), 0)

    def attend(query, result, tiles, counts, first=False, heads=None, clean=True):
        tile_count = len(counts)
        heads = range(width // HEAD) if heads is None else heads
        span = slice(0, width if len(heads) * HEAD == width else half_width)
        if heads[0] > 0:
            span = high
        for t in range(tile_count if clean else 0):
            live = (position[:, span] < counts[t]).astype(jnp.float32)
            tiles[t, 0, :, span] = (
                tiles[t, 0, :, span].astype(jnp.float32) * live
            ).astype(jnp.bfloat16)

        def one(block, carry):
            rows = pl.ds(pl.multiple_of(block * ROWS, ROWS), ROWS)
            for h in heads:
                cols = slice(h * HEAD, (h + 1) * HEAD)
                keys = tiles[:, 0, :, cols].reshape(tile_count * TILE, HEAD)
                values = tiles[:, 1, :, cols].reshape(tile_count * TILE, HEAD)
                scores = lax.dot_general(
                    query[rows, cols], keys, (((1,), (1,)), ((), ())),
                    preferred_element_type=jnp.float32,
                )
                weights = silu_half(scores * HALF_SCALE).astype(jnp.bfloat16)
                added = jnp.dot(weights, values, preferred_element_type=jnp.float32)
                result[rows, cols] = added if first else result[rows, cols] + added
            return carry

        lax.fori_loop(0, cands // ROWS, one, 0)

    def counts_of(ref):
        block = ref[...]
        return [block[1:2, k : k + 1] for k in range(depth)]

    for k in range(depth):
        own_tiles[k] = kv_ref[wanted_s[n - 1, 0, k]]
    attend(act.at[0], total, own_tiles, counts_of(table.at[me]))

    def from_all():
        for k in range(depth):
            counts = []
            for d in range(n - 1):
                tile_copy(k, d).wait_recv()
                counts.append(table[lax.rem(me + d + 1, n)][1:2, k : k + 1])
            attend(act.at[0], total, arrived.at[k], counts)

    def serve(mine, tiles, side, slot, cols, heads):
        for k in range(depth):
            own_tiles[k] = kv_ref[wanted_s[slot, 0, k]]
        query_copy(cols).wait_recv()
        attend(peer_query, peer_total, own_tiles, counts_of(mine), first=True, heads=heads)
        for k in range(depth):
            if cols is every:
                tile_copy(k, 1).wait_recv()
            else:
                low_copy(k).wait_recv()
        attend(peer_query, peer_total, tiles, counts_of(wanted.at[slot, side]), heads=heads)

        def narrow(block, carry):
            rows = pl.ds(pl.multiple_of(block * ROWS, ROWS), ROWS)
            partial_out[rows, cols] = peer_total[rows, cols].astype(jnp.bfloat16)
            return carry

        lax.fori_loop(0, cands // ROWS, narrow, 0)
        partial_copy(cols).start()

    def collect(cols):
        partial_copy(cols).wait_recv()

        def widen(block, carry):
            rows = pl.ds(pl.multiple_of(block * ROWS, ROWS), ROWS)
            total[rows, cols] += partial_in[rows, cols].astype(jnp.float32)
            return carry

        lax.fori_loop(0, cands // ROWS, widen, 0)

    def at_middle():
        side = 3 * (me - 1)
        serve(wanted.at[near, me], arrived.at[:, 1], side, near, every, None)
        for d in (0, 2):

            @pl.when(near == d)
            def _():
                for k in range(depth):
                    tile_copy(k, d).wait_recv()
                attend(act.at[0], total, arrived.at[:, d], counts_of(table.at[side]))

        collect(every)

    def at_edge():
        side = 1 + me // 3
        lows, highs = (0, 1), (2, 3)
        serve(wanted.at[facing, me], low_arrived, side, facing, low, lows)
        for k in range(depth):
            counts = []
            for d in range(n - 1):
                if d == 1:
                    tile_copy(k, d, high).wait_recv()
                else:
                    pl.when(facing == d)(tile_copy(k, d).wait_recv)
                    pl.when(facing != d)(tile_copy(k, d, high).wait_recv)
                counts.append(table[lax.rem(me + d + 1, n)][1:2, k : k + 1])
            attend(act.at[0], total, arrived.at[k], counts, heads=highs)
            for d in (0, 2):

                @pl.when(facing == d)
                def _():
                    attend(
                        act.at[0], total, arrived.at[k, d : d + 1], counts[d : d + 1], heads=lows
                    )

        collect(low)

    if split:
        pl.when(edge)(at_edge)
        pl.when(middle)(at_middle)
    else:
        from_all()

    gain_load.wait()

    def moments(block, carry):
        rows = pl.ds(pl.multiple_of(block * ROWS, ROWS), ROWS)
        attended = total[rows, :] * (1.0 / (HT * TILE + 1))
        sums = jnp.sum(attended, axis=1, keepdims=True)
        squares = jnp.sum(attended * attended, axis=1, keepdims=True)
        at = lax.broadcasted_iota(jnp.int32, (ROWS, 128), 1)
        stats[rows, :] = jnp.where(at < 64, sums, squares)
        return carry

    lax.fori_loop(0, cands // ROWS, moments, 0)
    stat_copy = pltpu.make_async_remote_copy(
        src_ref=stats,
        dst_ref=peer_stats,
        send_sem=stat_send,
        recv_sem=stat_recv,
        device_id={"rep": 1 - core},
        device_id_type=pl.DeviceIdType.MESH,
    )
    stat_copy.start()
    stat_copy.wait_recv()

    def finish(block, carry):
        rows = pl.ds(pl.multiple_of(block * ROWS, ROWS), ROWS)
        both = stats[rows, :] + peer_stats[rows, :]
        average = both[:, 0:1] * (1.0 / D)
        variance = both[:, 64:65] * (1.0 / D) - average * average
        attended = total[rows, :] * (1.0 / (HT * TILE + 1))
        normed = (attended - average) * lax.rsqrt(variance + 1e-05) * gain_ref[...]
        out_ref[0, rows, :] = (normed * act[3, rows, :].astype(jnp.float32)).astype(jnp.bfloat16)
        return carry

    lax.fori_loop(0, cands // ROWS, finish, 0)
    stat_copy.wait_send()
    for copy in list_copies:
        copy.wait_send()
    if split:
        for k in range(depth):
            for d in range(n - 1):
                sends(d, lambda d, cols, k=k: tile_copy(k, d, cols).wait_send())

        @pl.when(middle)
        def _():
            for k in range(depth):
                low_copy(k).wait_send()
            query_copy(every).wait_send()
            partial_copy(every).wait_send()

        @pl.when(edge)
        def _():
            query_copy(low).wait_send()
            partial_copy(low).wait_send()
    else:
        for k in range(depth):
            for d in range(n - 1):
                tile_copy(k, d).wait_send()


def local(candidates, kv_cache, tile_owner, tile_slot, tile_length, norm_gain):
    n = lax.axis_size("cache")
    depth = (HT - 2) // n + 2
    cands, width = candidates.shape[1], candidates.shape[3]
    vmem = pl.BlockSpec(memory_space=pltpu.VMEM)
    tile = (2, TILE, width)
    dma = pltpu.SemaphoreType.DMA
    return pl.pallas_call(
        functools.partial(kernel, n, depth, n == 4),
        out_shape=jax.ShapeDtypeStruct((1, cands, width), jnp.bfloat16),
        in_specs=[pl.BlockSpec(memory_space=pltpu.HBM)] * 6,
        out_specs=vmem,
        scratch_shapes=[
            pltpu.VMEM((cands, 4, width), jnp.bfloat16),
            pltpu.VMEM(kv_cache.shape, jnp.bfloat16),
            pltpu.VMEM((3, 1, HT), jnp.int32),
            pltpu.VMEM((1, width), jnp.float32),
            pltpu.VMEM((4, cands, width), jnp.bfloat16),
            pltpu.VMEM((cands, width), jnp.float32),
            pltpu.VMEM((cands, 128), jnp.float32),
            pltpu.VMEM((cands, 128), jnp.float32),
            pltpu.VMEM((n, 8, 128), jnp.int32),
            pltpu.VMEM((n - 1, n, 8, 128), jnp.int32),
            pltpu.SMEM((n, 8, 128), jnp.int32),
            pltpu.VMEM((depth,) + tile, jnp.bfloat16),
            pltpu.VMEM((depth, n - 1) + tile, jnp.bfloat16),
            pltpu.VMEM((depth, n - 1) + tile, jnp.bfloat16),
            pltpu.VMEM((cands, width), jnp.bfloat16),
            pltpu.VMEM((cands, width), jnp.float32),
            pltpu.VMEM((cands, width), jnp.bfloat16),
            pltpu.VMEM((cands, width), jnp.bfloat16),
            pltpu.VMEM((depth, 2, TILE, width // 2), jnp.bfloat16),
            dma((6,)),
            dma((n - 1,)),
            dma((n - 1,)),
            dma((n,)),
            dma((depth, n - 1)),
            dma((depth, n - 1)),
            dma,
            dma,
            dma,
            dma,
            dma,
            dma,
            dma((depth,)),
            dma((depth,)),
        ],
        compiler_params=pltpu.CompilerParams(
            collective_id=0, has_side_effects=True, vmem_limit_bytes=60 * 1024 * 1024
        ),
        cost_estimate=pl.CostEstimate(
            flops=4 * cands * width * HT * TILE, bytes_accessed=5 * 2**20, transcendentals=0
        ),
    )(candidates, kv_cache, tile_owner, tile_slot, tile_length, norm_gain[None])


def solution(mesh):
    placed = (
        P(("groups", "cache", "req"), None, None, "rep"),
        P(("groups", "cache", "req"), None, None, "rep"),
        P(("groups", "cache", "req"), None),
        P(("groups", "cache", "req"), None),
        P(("groups", "cache", "req"), None),
        P("rep"),
    )
    return jax.shard_map(
        local,
        mesh=mesh,
        in_specs=placed,
        out_specs=P(("groups", "cache", "req"), None, "rep"),
        check_vma=False,
    )
```
